128 devices in a mesh: replica: 8 (over z, x_lo), dp: 2 (over x_hi), tensor: 8 (over y, core).
Axes of the slice: x: 4 (x_hi: 2, x_lo: 2; x = x_hi * 2 + x_lo), y: 4, z: 4, core: 2. Of those that a mesh axis runs over, the one named last changes fastest.
Arguments:
- tokens: bfloat16 [8, 2048, 2048], P('replica', 'dp', 'tensor'), may hold values from -6 to 6
- grad_out: bfloat16 [8, 2048, 14336], P('replica', 'dp', 'tensor'), may hold values from -250 to 250, as said below
- weights: bfloat16 [8, 2048, 14336], P('replica', 'dp', 'tensor'), may hold values from -6 to 6
- first_moment: bfloat16 [8, 2048, 14336], P('replica', 'dp', 'tensor'), may hold values from -4 to 4
- second_moment: bfloat16 [8, 2048, 14336], P('replica', 'dp', 'tensor'), may hold values from 0.019897461 to 0.19921875
Outputs:
- new_weights: bfloat16 [8, 2048, 14336], P('replica', 'dp', 'tensor')
- new_first: bfloat16 [8, 2048, 14336], P('replica', 'dp', 'tensor')
- new_second: bfloat16 [8, 2048, 14336], P('replica', 'dp', 'tensor')
The draws below stay inside these ranges and needn't reach their ends.
Inputs may be any that keep to these rules, and one draw needn't show every extreme that they name: `grad_out`: the upstream gradient.
All inputs are finite; a program needn't handle non-finite values.
Results may differ from the reference program's by a relative error of at most 0.0051.
Values may be sent and summed in bfloat16 or wider, within the bound.
No kernel may reach another device: no remote copies, remote signals or barrier semaphores. Data moves between devices by JAX's collectives and lax.ppermute only.
A program may use at most 192 MiB of HBM per device.

```python
import math
import jax
import jax.numpy as jnp
from jax import lax

D = 2048
FF = 14336
TOK_DEV = 1024
STEP = 1
ROWS = 2048
N_REPLICA = 8
N_DP = 2


def draw_grad_out(key, part):
    key = jax.random.fold_in(key, 7)
    key_base, key_cols, key_rows, key_pick = jax.random.split(key, 4)
    shape = (N_REPLICA, N_DP * TOK_DEV, FF)
    position = jnp.arange(FF, dtype=jnp.float32) / FF
    jitter = jax.random.uniform(key_cols, (FF,), jnp.float32, math.log(0.7), math.log(1.4))
    col_scale = jnp.exp(math.log(10.0) * position + jitter)
    order = jax.random.permutation(key_pick, N_REPLICA)
    quiet = order < max(1, N_REPLICA // 4)
    group_scale = jnp.where(quiet, 0.01 / math.sqrt(N_DP * TOK_DEV), 1.0).astype(jnp.float32)[:, None, None]
    base = jnp.clip(jax.random.normal(key_base, shape, jnp.float32), -4.0, 4.0)
    row_scale = jnp.exp(jax.random.uniform(key_rows, (N_REPLICA, N_DP * TOK_DEV, 1), jnp.float32, 0.0, math.log(3.0)))
    return (base * row_scale * col_scale[None, None, :] * group_scale).astype(jnp.bfloat16)


def shard_levels(own_key, shape, cuts, least, largest):
    loudness, own = 1.0, jax.random.fold_in(own_key, 6)
    for dim, parts in cuts:
        heights = jnp.exp(jax.random.uniform(jax.random.fold_in(own, dim), (parts,), jnp.float32, least / len(cuts), largest / len(cuts)))
        loudness = loudness * jnp.repeat(heights, shape[dim] // parts).reshape([-1 if axis == dim else 1 for axis in range(len(shape))])
    return loudness


def centred(own_key, extent, scale, reach, cuts=(), kind=jnp.bfloat16):
    entries = scale * jax.random.normal(own_key, extent, jnp.float32)
    if cuts:
        entries = entries * shard_levels(own_key, extent, cuts, -0.22, 0.18)
    return jnp.clip(entries, -reach, reach).astype(kind)


def setup_inputs(seed: int = 0) -> dict:
    key_of = jax.random.split(jax.random.key(seed), 6)
    return {
        "tokens": centred(key_of[0], (N_REPLICA, ROWS, D), 1.0, 6.0, ((0, 8), (1, 2), (2, 8))),
        "grad_out": draw_grad_out(jax.random.fold_in(key_of[5], 71), 0),
        "weights": centred(key_of[2], (N_REPLICA, D, FF), 1.0, 6.0, ((0, 8), (1, 2), (2, 8))),
        "first_moment": centred(key_of[3], (N_REPLICA, D, FF), 0.3, 4.0, ((0, 8), (1, 2), (2, 8))),
        "second_moment": jnp.clip(jnp.exp(math.log(0.19921875) - 2.3038113 * jax.random.uniform(key_of[4], (N_REPLICA, D, FF), jnp.float32) ** shard_levels(key_of[4], (N_REPLICA, D, FF), ((0, 8), (1, 2), (2, 8)), -0.2, 0.2)), 0.019897461, 0.19921875).astype(jnp.bfloat16),
    }


def adamw(grad, total, weights, first_moment, second_moment):
    clip = jnp.minimum(1.0, 1.0 / jnp.sqrt(total / (D * FF) + 1e-06))
    scaled = clip * grad
    moment_one = 0.9 * first_moment.astype(jnp.float32) + 0.1 * scaled
    moment_two = 0.95 * second_moment.astype(jnp.float32) + 0.05 * scaled * scaled
    fix_one = 1.0 - 0.9 ** STEP
    fix_two = 1.0 - 0.95 ** STEP
    update = moment_one / fix_one / (jnp.sqrt(moment_two / fix_two) + 1e-08)
    old = weights.astype(jnp.float32)
    fresh = old - 0.05 * (update + 0.1 * old)
    return jnp.stack([fresh.astype(jnp.bfloat16), moment_one.astype(jnp.bfloat16), moment_two.astype(jnp.bfloat16)])

def reference(tokens, grad_out, weights, first_moment, second_moment):

    def one_group(item):
        inputs, upstream, params, moment_one, moment_two = item
        grad = jnp.dot(inputs.T, upstream, preferred_element_type=jnp.float32)
        total = jnp.sum(grad * grad)
        return adamw(grad, total, params, moment_one, moment_two)
    states = lax.map(one_group, (tokens, grad_out, weights, first_moment, second_moment))
    partner = jnp.roll(states, N_REPLICA // 2, axis=0)
    mixed = (0.5 * (states.astype(jnp.float32) + partner.astype(jnp.float32))).astype(jnp.bfloat16)
    return (mixed[:, 0], mixed[:, 1], mixed[:, 2])
```

```python
import jax
import jax.numpy as jnp
from jax import lax
from jax.experimental import pallas as pl
from jax.experimental.pallas import tpu as pltpu
from jax.sharding import PartitionSpec as P

D = 2048
FF = 14336
STEP = 1
COLS = 256
FIX_ONE = 1.0 - 0.9**STEP
FIX_TWO = 1.0 - 0.95**STEP
BF16 = jnp.bfloat16
F32 = jnp.float32


def across(value):
    return lax.ppermute(value, "replica", [(s, s ^ 4) for s in range(8)])


def swap_dp(value):
    return lax.ppermute(value, "dp", [(0, 1), (1, 0)])


def gather_tokens(mine):
    pairs = []
    for d in range(2):
        for t in range(8):
            stays = t // 4 == d
            pairs.append((d * 8 + t, d * 8 + t if stays else (1 - d) * 8 + (t ^ 4)))
    moved = lax.ppermute(mine, ("dp", "tensor"), pairs)
    return lax.all_gather(moved, "tensor", axis=0, tiled=False)


def group_sum(value):
    for bit in (1, 2, 4):
        value = value + lax.ppermute(value, "tensor", [(t, t ^ bit) for t in range(8)])
    return value + swap_dp(value)


def clip_of(total_ref):
    total = jnp.sum(total_ref[...], keepdims=True)
    return jnp.minimum(1.0, 1.0 / jnp.sqrt(total / (D * FF) + 1e-06))


def moments(scaled, first, second):
    one = 0.9 * first.astype(F32) + 0.1 * scaled
    two = 0.95 * second.astype(F32) + 0.05 * scaled * scaled
    return one.astype(BF16), two.astype(BF16)


def stepped(old, one, two):
    old = old.astype(F32)
    one = one.astype(F32)
    two = two.astype(F32)
    update = one / FIX_ONE / (jnp.sqrt(two / FIX_TWO) + 1e-08)
    return (old - 0.05 * (update + 0.1 * old)).astype(BF16)


def mean(a, b):
    return (0.5 * (a.astype(F32) + b.astype(F32))).astype(BF16)


def make_kernel(total_ref, grad_ref, first_ref, second_ref, out_ref):
    one, two = moments(clip_of(total_ref) * grad_ref[...], first_ref[...], second_ref[...])
    out_ref[0] = one
    out_ref[1] = two


def make(total, grad, first, second, chunk):
    rows = grad.shape[0]
    step = 256
    wide = pl.BlockSpec((step, COLS), lambda i: (i, chunk))
    return pl.pallas_call(
        make_kernel,
        grid=(rows // step,),
        out_shape=jax.ShapeDtypeStruct((2, rows, COLS), BF16),
        in_specs=[
            pl.BlockSpec((8, 128), lambda i: (0, 0)),
            pl.BlockSpec((step, COLS), lambda i: (i, 0)),
            wide,
            wide,
        ],
        out_specs=pl.BlockSpec((2, step, COLS), lambda i: (0, i, 0)),
        cost_estimate=pl.CostEstimate(flops=10 * rows * COLS, bytes_accessed=12 * rows * COLS, transcendentals=0),
    )(total, grad, first, second)


def mix_kernel(mine_ref, other_ref, old_ref, old_other_ref, *rest):
    w_ref, one_ref, two_ref = rest[-3:]
    one, two = mine_ref[0], mine_ref[1]
    one_other, two_other = other_ref[0], other_ref[1]
    w_ref[...] = mean(stepped(old_ref[...], one, two), stepped(old_other_ref[...], one_other, two_other))
    one_ref[...] = mean(one, one_other)
    two_ref[...] = mean(two, two_other)


def mix(mine, other, old, old_other, chunk, outs):
    rows, cols = old.shape
    step = 256
    wide = pl.BlockSpec((step, COLS), lambda i: (i, chunk))
    pair = pl.BlockSpec((2, step, COLS), lambda i: (0, i, 0))
    shape = jax.ShapeDtypeStruct((rows, cols), BF16)
    return pl.pallas_call(
        mix_kernel,
        grid=(rows // step,),
        out_shape=(shape, shape, shape),
        in_specs=[pair, pair, wide, wide] + [pl.BlockSpec(memory_space=pl.ANY)] * len(outs),
        out_specs=(wide, wide, wide),
        input_output_aliases={4 + i: i for i in range(len(outs))},
        cost_estimate=pl.CostEstimate(flops=40 * rows * COLS, bytes_accessed=18 * rows * COLS, transcendentals=2 * rows * COLS),
    )(mine, other, old, old_other, *outs)


def first_mix_kernel(total_ref, total_other_ref, grad_ref, grad_other_ref, first_ref, first_other_ref, second_ref, second_other_ref, old_ref, old_other_ref, w_ref, one_ref, two_ref):
    one, two = moments(clip_of(total_ref) * grad_ref[...], first_ref[...], second_ref[...])
    scaled = clip_of(total_other_ref) * grad_other_ref[...].astype(F32)
    one_other, two_other = moments(scaled, first_other_ref[...], second_other_ref[...])
    w_ref[...] = mean(stepped(old_ref[...], one, two), stepped(old_other_ref[...], one_other, two_other))
    one_ref[...] = mean(one, one_other)
    two_ref[...] = mean(two, two_other)


def first_mix(total, total_other, grad, grad_other, first, first_other, second, second_other, old, old_other, chunk):
    rows, cols = old.shape
    step = 256
    wide = pl.BlockSpec((step, COLS), lambda i: (i, chunk))
    thin = pl.BlockSpec((step, COLS), lambda i: (i, 0))
    whole = pl.BlockSpec((8, 128), lambda i: (0, 0))
    shape = jax.ShapeDtypeStruct((rows, cols), BF16)
    return pl.pallas_call(
        first_mix_kernel,
        grid=(rows // step,),
        out_shape=(shape, shape, shape),
        in_specs=[whole, whole, thin, thin, wide, thin, wide, thin, wide, wide],
        out_specs=(wide, wide, wide),
        cost_estimate=pl.CostEstimate(flops=60 * rows * COLS, bytes_accessed=22 * rows * COLS, transcendentals=2 * rows * COLS),
    )(total, total_other, grad, grad_other, first, first_other, second, second_other, old, old_other)


def body(tokens, grad_out, weights, first_moment, second_moment):
    upstream, old = grad_out[0], weights[0]
    first, second = first_moment[0], second_moment[0]
    rows, cols = old.shape
    chunks = cols // COLS
    part = lambda array, c: array[:, c * COLS : (c + 1) * COLS]

    features = gather_tokens(tokens[0])
    up_other = [swap_dp(part(upstream, c)) for c in range(chunks)]
    old_other = across(old)
    first_other = across(part(first, 0))
    second_other = across(part(second, 0))

    d = lax.axis_index("dp")
    mine = lax.dynamic_slice_in_dim(features, d * 4, 4, 0)
    theirs = lax.dynamic_slice_in_dim(features, (1 - d) * 4, 4, 0)

    def product(x, u):
        return lax.dot_general(x, u, (((1,), (0,)), ((), ())), preferred_element_type=F32).reshape(rows, -1)

    local = product(mine, upstream)
    grads, squares = [], jnp.zeros((8, 128), F32)
    for c in range(chunks):
        grad = part(local, c) + product(theirs, up_other[c])
        grads.append(grad)
        squares = squares + jnp.sum((grad * grad).reshape(rows // 8, 8, COLS // 128, 128), axis=(0, 2))
    grad_other = across(grads[0].astype(BF16))
    total = group_sum(squares)
    total_other = across(total)

    sent, received = [None], [None]
    for c in range(1, chunks):
        sent.append(make(total, grads[c], first, second, c))
        received.append(across(sent[c]))
    outs = first_mix(total, total_other, grads[0], grad_other, first, first_other, second, second_other, old, old_other, 0)
    for c in range(1, chunks):
        outs = mix(sent[c], received[c], old, old_other, c, outs)
    return tuple(out[None] for out in outs)


def solution(mesh):
    placed = P("replica", "dp", "tensor")
    return jax.shard_map(
        body,
        mesh=mesh,
        in_specs=(placed,) * 5,
        out_specs=(placed,) * 3,
        check_vma=False,
    )
```

```python
import jax
import jax.numpy as jnp
from jax import lax
from jax.experimental import pallas as pl
from jax.experimental.pallas import tpu as pltpu
from jax.sharding import PartitionSpec as P

D = 2048
FF = 14336
STEP = 1
FIX_ONE = 1.0 - 0.9**STEP
FIX_TWO = 1.0 - 0.95**STEP
BF16 = jnp.bfloat16
ANYWHERE = pl.BlockSpec(memory_space=pl.ANY)
F32 = jnp.float32


def across(value):
    return lax.ppermute(value, "replica", [(s, s ^ 4) for s in range(8)])


def swap_dp(value):
    return lax.ppermute(value, "dp", [(0, 1), (1, 0)])


def nothing_kernel(*refs):
    del refs


def corner(value):
    return pl.BlockSpec((1,) * (value.ndim - 2) + (16 if value.dtype == BF16 else 8, 128), lambda i: (0,) * value.ndim)


def gate(values, earlier):
    return pl.pallas_call(
        nothing_kernel,
        grid=(1,),
        out_shape=[jax.ShapeDtypeStruct(value.shape, value.dtype) for value in values],
        in_specs=[ANYWHERE] * len(values) + [corner(value) for value in earlier],
        out_specs=[ANYWHERE] * len(values),
        input_output_aliases={i: i for i in range(len(values))},
        cost_estimate=pl.CostEstimate(flops=0, bytes_accessed=4096, transcendentals=0),
    )(*values, *earlier)


def turned(value, bits):
    return lax.ppermute(value, "tensor", [(t, t ^ bits) for t in range(8)])


def settle(mine):
    pairs = []
    for d in range(2):
        for t in range(8):
            stays = t // 4 == d
            pairs.append((d * 8 + t, d * 8 + t if stays else (1 - d) * 8 + (t ^ 4)))
    return lax.ppermute(mine, ("dp", "tensor"), pairs)


def along_y(value):
    copies = jnp.broadcast_to(value, (4, *value.shape))
    return lax.all_to_all(copies, "tensor", 0, 0, tiled=True, axis_index_groups=[[0, 2, 4, 6], [1, 3, 5, 7]])


def assemble_kernel(slot_ref, near_ref, far_ref, out_ref):
    for k in range(4):
        out_ref[slot_ref[k]] = near_ref[k]
        out_ref[slot_ref[4 + k]] = far_ref[k]


def assemble(near, far):
    core = lax.axis_index("tensor") % 2
    flip = 4 * lax.axis_index("dp")
    slots = jnp.stack([(2 * y + core) ^ flip for y in range(4)] + [(2 * y + 1 - core) ^ flip for y in range(4)])
    whole = pl.BlockSpec(memory_space=pltpu.VMEM)
    return pl.pallas_call(
        assemble_kernel,
        out_shape=jax.ShapeDtypeStruct((8, *near.shape[1:]), BF16),
        in_specs=[pl.BlockSpec(memory_space=pltpu.SMEM), whole, whole],
        out_specs=whole,
        cost_estimate=pl.CostEstimate(flops=0, bytes_accessed=8 * near.size, transcendentals=0),
        compiler_params=pltpu.CompilerParams(vmem_limit_bytes=24 * 2**20),
    )(slots.astype(jnp.int32), near, far)


def group_sum(value):
    for bits in (1, 2, 4):
        value = value + turned(value, bits)
    return value + swap_dp(value)


def clip_of(total_ref):
    total = jnp.sum(total_ref[...], keepdims=True)
    return jnp.minimum(1.0, 1.0 / jnp.sqrt(total / (D * FF) + 1e-06))


def moments(scaled, first, second):
    one = 0.9 * first.astype(F32) + 0.1 * scaled
    two = 0.95 * second.astype(F32) + 0.05 * scaled * scaled
    return one.astype(BF16), two.astype(BF16)


def stepped(old, one, two):
    old = old.astype(F32)
    update = (one.astype(F32) * (1.0 / FIX_ONE)) / (jnp.sqrt(two.astype(F32) * (1.0 / FIX_TWO)) + 1e-08)
    return (old - 0.05 * (update + 0.1 * old)).astype(BF16)


def mean(a, b):
    return (0.5 * (a.astype(F32) + b.astype(F32))).astype(BF16)


def make_kernel(total_ref, grad_ref, first_ref, second_ref, old_ref, pair_ref, step_ref):
    one, two = moments(clip_of(total_ref) * grad_ref[...], first_ref[...], second_ref[...])
    pair_ref[0] = one
    pair_ref[1] = two
    step_ref[...] = stepped(old_ref[...], one, two)


def mix_kernel(pair_ref, step_ref, pair_other_ref, old_other_ref, *rest):
    w_ref, one_ref, two_ref, flag_ref = rest[-4:]
    flag_ref[...] = jnp.zeros_like(flag_ref)
    one_other, two_other = pair_other_ref[0], pair_other_ref[1]
    w_ref[...] = mean(step_ref[...], stepped(old_other_ref[...], one_other, two_other))
    one_ref[...] = mean(pair_ref[0], one_other)
    two_ref[...] = mean(pair_ref[1], two_other)


def early_kernel(
    total_ref,
    grad_ref,
    scaled_other_ref,
    first_ref,
    second_ref,
    first_other_ref,
    second_other_ref,
    old_ref,
    old_other_ref,
    *rest,
):
    w_ref, one_ref, two_ref = rest[-3:]
    one, two = moments(clip_of(total_ref) * grad_ref[...], first_ref[...], second_ref[...])
    scaled_other = scaled_other_ref[...].astype(F32)
    one_other, two_other = moments(scaled_other, first_other_ref[...], second_other_ref[...])
    w_ref[...] = mean(stepped(old_ref[...], one, two), stepped(old_other_ref[...], one_other, two_other))
    one_ref[...] = mean(one, one_other)
    two_ref[...] = mean(two, two_other)


STEP_ROWS = 512
TOTAL = pl.BlockSpec((8, 128), lambda i: (0, 0))


def columns(width, at=0):
    return pl.BlockSpec((STEP_ROWS, width), lambda i: (i, at // width))


def pair_of(width):
    return pl.BlockSpec((2, STEP_ROWS, width), lambda i: (0, i, 0))


def cost(rows, width, flops, size):
    return pl.CostEstimate(flops=flops * rows * width, bytes_accessed=size * rows * width, transcendentals=0)


def make(total, grad, within, first, second, old, at, width):
    rows = grad.shape[0]
    wide = columns(width, at)
    return pl.pallas_call(
        make_kernel,
        grid=(rows // STEP_ROWS,),
        out_shape=(jax.ShapeDtypeStruct((2, rows, width), BF16), jax.ShapeDtypeStruct((rows, width), BF16)),
        in_specs=[TOTAL, columns(width, within), wide, wide, wide],
        out_specs=(pair_of(width), columns(width)),
        cost_estimate=cost(rows, width, 30, 16),
    )(total, grad, first, second, old)


def mix(pair, step, pair_other, old_other, at, within, width, shape, outs):
    rows = shape[0]
    wide = columns(width, at)
    whole = jax.ShapeDtypeStruct(shape, BF16)
    return pl.pallas_call(
        mix_kernel,
        grid=(rows // STEP_ROWS,),
        out_shape=(whole, whole, whole, jax.ShapeDtypeStruct((8, 128), F32)),
        in_specs=[pair_of(width), columns(width), pair_of(width), columns(width, within)] + [ANYWHERE] * len(outs),
        out_specs=(wide, wide, wide, TOTAL),
        input_output_aliases={4 + i: i for i in range(len(outs))},
        cost_estimate=cost(rows, width, 30, 18),
    )(pair, step, pair_other, old_other, *outs)


def early(total, grad, scaled_other, first, second, other, old, old_other, width, outs):
    rows, cols = old.shape
    wide = columns(width)
    shape = jax.ShapeDtypeStruct((rows, cols), BF16)
    return pl.pallas_call(
        early_kernel,
        grid=(rows // STEP_ROWS,),
        out_shape=(shape, shape, shape),
        in_specs=[TOTAL] + [wide] * 5 + [columns(width, width), wide, wide] + [ANYWHERE] * 3,
        out_specs=(wide, wide, wide),
        input_output_aliases={9 + i: i for i in range(3)},
        cost_estimate=cost(rows, width, 60, 22),
    )(total, grad, scaled_other, first, second, other, other, old, old_other, *outs)


def scale_kernel(total_ref, grad_ref, out_ref):
    out_ref[...] = (clip_of(total_ref) * grad_ref[...]).astype(BF16)


def scale(total, grad, width):
    rows = grad.shape[0]
    return pl.pallas_call(
        scale_kernel,
        grid=(rows // STEP_ROWS,),
        out_shape=jax.ShapeDtypeStruct((rows, width), BF16),
        in_specs=[TOTAL, columns(width)],
        out_specs=columns(width),
        cost_estimate=cost(rows, width, 2, 6),
    )(total, grad)


def finish_kernel(x_ref, u_ref, local_ref, grad_ref, squares_ref):
    grad = local_ref[...] + jnp.dot(x_ref[0], u_ref[...], preferred_element_type=F32)
    grad_ref[...] = grad
    width = grad.shape[1]
    square = grad * grad
    lanes = sum(square[:, k : k + 128] for k in range(0, width, 128))

    @pl.when(pl.program_id(0) == 0)
    def _():
        squares_ref[...] = jnp.zeros_like(squares_ref)

    squares_ref[...] += jnp.sum(lanes.reshape(-1, 8, 128), axis=0)


def finish(x, u, local, piece):
    blocks, step, depth = x.shape
    at, width = piece
    return pl.pallas_call(
        finish_kernel,
        grid=(blocks,),
        out_shape=(jax.ShapeDtypeStruct((blocks * step, width), F32), jax.ShapeDtypeStruct((8, 128), F32)),
        in_specs=[
            pl.BlockSpec((1, step, depth), lambda i: (i, 0, 0)),
            pl.BlockSpec((depth, width), lambda i: (0, 0)),
            pl.BlockSpec((step, width), lambda i: (i, at // width)),
        ],
        out_specs=(pl.BlockSpec((step, width), lambda i: (i, 0)), pl.BlockSpec((8, 128), lambda i: (0, 0))),
        cost_estimate=pl.CostEstimate(flops=2 * blocks * step * depth * width, bytes_accessed=10 * blocks * step * width, transcendentals=0),
        compiler_params=pltpu.CompilerParams(vmem_limit_bytes=32 * 2**20),
    )(x, u, local)


EARLY = 256
UP = ((1536, 256), (0, 1024), (1024, 512))
OLD = ((0, 1280), (1280, 512))
LATE = ((256, 256), (512, 256), (768, 256), (1024, 256), (1280, 256), (1536, 128), (1664, 128))


def part(value, piece):
    return value[:, piece[0] : piece[0] + piece[1]]


def holder(pieces, at):
    index = next(i for i, (start, width) in enumerate(pieces) if start <= at < start + width)
    return index, at - pieces[index][0]


def body(tokens, grad_out, weights, first_moment, second_moment):
    upstream, old = grad_out[0], weights[0]
    first, second = first_moment[0], second_moment[0]
    rows = old.shape[0]

    settled = settle(tokens[0])
    up_other = [swap_dp(part(upstream, piece)) for piece in UP[:2]]
    old_other = [across(part(old, OLD[0]))]

    (settled,) = gate((settled,), (up_other[0],))
    near = along_y(settled)
    last = jnp.concatenate([first[:, :EARLY], second[:, :EARLY], part(old, OLD[1])], axis=1)
    near, up_last, last = gate((near, part(upstream, UP[2]), last), (up_other[1], old_other[0]))
    far = turned(near, 1)
    up_other.append(swap_dp(up_last))
    old_other.append(across(last))

    features = assemble(near, far)
    local = lax.dot_general(features[:4], upstream, (((1,), (0,)), ((), ())), preferred_element_type=F32).reshape(rows, -1)
    turned_features = jnp.swapaxes(features[4:], 1, 2)
    grads, squares = [], jnp.zeros((8, 128), F32)
    for piece, other in zip(UP, up_other):
        grad, square = finish(turned_features, other, local, piece)
        grads.append(grad)
        squares = squares + square
    total = group_sum(squares)

    scaled = scale(total, grads[1], EARLY)
    scaled_other = across(scaled)
    pairs, steps, received, flags = [], [], [scaled_other], []
    outs = ()
    for i in range(len(LATE) + 3):
        if i < len(LATE):
            at, width = LATE[i]
            chunk, within = holder(UP, at)
            pair, step = make(total, grads[chunk], within, first, second, old, at, width)
            (pair,) = gate((pair,), (received[i - 2] if i >= 2 else old_other[1],) + ((flags[i - 4],) if i >= 4 else ()))
            pairs.append(pair)
            steps.append(step)
            received.append(across(pair))
        if i >= 3:
            j = i - 3
            at, width = LATE[j]
            chunk, within = holder(OLD, at)
            within += 2 * EARLY * chunk
            *outs, flag = mix(pairs[j], steps[j], received[j + 1], old_other[chunk], at, within, width, old.shape, outs)
            flags.append(flag)
        if i == 3:
            outs = early(total, grads[1], scaled_other, first, second, old_other[1], old, old_other[0], EARLY, outs)
    return tuple(out[None] for out in outs)


def solution(mesh):
    placed = P("replica", "dp", "tensor")
    return jax.shard_map(
        body,
        mesh=mesh,
        in_specs=(placed,) * 5,
        out_specs=(placed,) * 3,
        check_vma=False,
    )
```

```python
import jax
import jax.numpy as jnp
from jax import lax
from jax.experimental import pallas as pl
from jax.experimental.pallas import tpu as pltpu
from jax.sharding import PartitionSpec as P

D = 2048
FF = 14336
STEP = 1
FIX_ONE = 1.0 - 0.9**STEP
FIX_TWO = 1.0 - 0.95**STEP
BF16 = jnp.bfloat16
ANYWHERE = pl.BlockSpec(memory_space=pl.ANY)
SLIGHT = pl.CostEstimate(flops=0, bytes_accessed=4096, transcendentals=0)
F32 = jnp.float32


def across(value):
    return lax.ppermute(value, "replica", [(s, s ^ 4) for s in range(8)])


def swap_dp(value):
    return lax.ppermute(value, "dp", [(0, 1), (1, 0)])


def nothing_kernel(*refs):
    del refs


def corner(value):
    if value.ndim > 2:
        return pl.BlockSpec(memory_space=pltpu.VMEM)
    return pl.BlockSpec((1,) * (value.ndim - 2) + (16 if value.dtype == BF16 else 8, 128), lambda i: (0,) * value.ndim)


def gate(values, earlier, size=4096):
    return pl.pallas_call(
        nothing_kernel,
        grid=(1,),
        out_shape=[jax.ShapeDtypeStruct(value.shape, value.dtype) for value in values],
        in_specs=[ANYWHERE] * len(values) + [corner(value) for value in earlier],
        out_specs=[ANYWHERE] * len(values),
        input_output_aliases={i: i for i in range(len(values))},
        cost_estimate=pl.CostEstimate(flops=0, bytes_accessed=size, transcendentals=0),
    )(*values, *earlier)


def turned(value, bits):
    return lax.ppermute(value, "tensor", [(t, t ^ bits) for t in range(8)])


def settle(mine):
    pairs = []
    for d in range(2):
        for t in range(8):
            stays = t // 4 == d
            pairs.append((d * 8 + t, d * 8 + t if stays else (1 - d) * 8 + (t ^ 6)))
    return lax.ppermute(mine, ("dp", "tensor"), pairs)


def along_y(value):
    copies = jnp.broadcast_to(value, (4, *value.shape))
    return lax.all_to_all(copies, "tensor", 0, 0, tiled=True, axis_index_groups=[[0, 2, 4, 6], [1, 3, 5, 7]])


def assemble_kernel(slot_ref, near_ref, low_ref, high_ref, out_ref):
    for k in range(4):
        out_ref[slot_ref[k]] = near_ref[k]
    for k in range(2):
        out_ref[slot_ref[4 + k]] = low_ref[k]
        out_ref[slot_ref[6 + k]] = high_ref[k]


def assemble(near, low, high):
    core = lax.axis_index("tensor") % 2
    flip = 4 * lax.axis_index("dp")
    places = jnp.stack([(2 * y + core) ^ flip for y in range(4)] + [(2 * y + 1 - core) ^ flip for y in range(4)])
    slots = places ^ (places // 4 * 2)
    whole = pl.BlockSpec(memory_space=pltpu.VMEM)
    return pl.pallas_call(
        assemble_kernel,
        out_shape=jax.ShapeDtypeStruct((8, *near.shape[1:]), BF16),
        in_specs=[pl.BlockSpec(memory_space=pltpu.SMEM)] + [whole] * 3,
        out_specs=whole,
        cost_estimate=SLIGHT,
        compiler_params=pltpu.CompilerParams(vmem_limit_bytes=24 * 2**20),
    )(slots.astype(jnp.int32), near, low, high)


def add_kernel(one_ref, two_ref, *rest):
    rest[-1][...] = one_ref[...] + two_ref[...]


def group_sum(value, earlier):
    value = value + turned(value, 1)
    value = value + turned(value, 2) + turned(value, 4) + turned(value, 6)
    return pl.pallas_call(
        add_kernel,
        grid=(1,),
        out_shape=jax.ShapeDtypeStruct(value.shape, F32),
        in_specs=[corner(value)] * 2 + [corner(item) for item in earlier],
        out_specs=corner(value),
        cost_estimate=SLIGHT,
    )(value, swap_dp(value), *earlier)


def clip_of(total_ref):
    total = jnp.sum(total_ref[...], keepdims=True)
    return jnp.minimum(1.0, 1.0 / jnp.sqrt(total / (D * FF) + 1e-06))


def moments(scaled, first, second):
    one = 0.9 * first.astype(F32) + 0.1 * scaled
    two = 0.95 * second.astype(F32) + 0.05 * scaled * scaled
    return one.astype(BF16), two.astype(BF16)


def stepped(old, one, two):
    old = old.astype(F32)
    update = (one.astype(F32) * (1.0 / FIX_ONE)) / (jnp.sqrt(two.astype(F32) * (1.0 / FIX_TWO)) + 1e-08)
    return (old - 0.05 * (update + 0.1 * old)).astype(BF16)


def mean(a, b):
    return (0.5 * (a.astype(F32) + b.astype(F32))).astype(BF16)


def make_kernel(total_ref, grad_ref, first_ref, second_ref, old_ref, pair_ref, step_ref):
    one, two = moments(clip_of(total_ref) * grad_ref[...], first_ref[...], second_ref[...])
    pair_ref[0] = one
    pair_ref[1] = two
    step_ref[...] = stepped(old_ref[...], one, two)


def make_first_kernel(total_ref, grad_ref, first_ref, second_ref, old_ref, pair_ref, step_ref):
    rows = grad_ref.shape[0]
    clip = clip_of(total_ref)
    one, two = moments(clip * grad_ref[...], first_ref[...], second_ref[...])
    pair_ref[0, :rows] = one
    pair_ref[1, :rows] = two
    step_ref[...] = stepped(old_ref[...], one, two)
    clip = jnp.broadcast_to(clip, (16, grad_ref.shape[1]))
    high = clip.astype(BF16)
    pair_ref[0, rows:] = high
    pair_ref[1, rows:] = (clip - high.astype(F32)).astype(BF16)


def make_first(total, grad, within, first, second, old, at, width):
    rows = grad.shape[0]
    chosen = lambda start: pl.BlockSpec((rows, width), lambda i: (0, start // width))
    return pl.pallas_call(
        make_first_kernel,
        grid=(1,),
        out_shape=(jax.ShapeDtypeStruct((2, rows + 16, width), BF16), jax.ShapeDtypeStruct((rows, width), BF16)),
        in_specs=[TOTAL, chosen(within), chosen(at), chosen(at), chosen(at)],
        out_specs=(pl.BlockSpec((2, rows + 16, width), lambda i: (0, 0, 0)), chosen(0)),
        cost_estimate=cost(rows, width, 30, 16),
        compiler_params=pltpu.CompilerParams(vmem_limit_bytes=56 * 2**20),
    )(total, grad, first, second, old)


def mix_kernel(pair_ref, step_ref, pair_other_ref, old_other_ref, *rest):
    w_ref, one_ref, two_ref, flag_ref = rest[-4:]
    flag_ref[...] = jnp.zeros_like(flag_ref)
    depth = step_ref.shape[0]
    here = pl.ds(pl.multiple_of(pl.program_id(0) * depth, depth), depth)
    one_other, two_other = pair_other_ref[0, here], pair_other_ref[1, here]
    w_ref[...] = mean(step_ref[...], stepped(old_other_ref[...], one_other, two_other))
    one_ref[...] = mean(pair_ref[0], one_other)
    two_ref[...] = mean(pair_ref[1], two_other)


def early_kernel(
    total_ref,
    clip_other_ref,
    grad_ref,
    grad_other_ref,
    first_ref,
    second_ref,
    first_other_ref,
    second_other_ref,
    old_ref,
    old_other_ref,
    *rest,
):
    w_ref, one_ref, two_ref = rest[-3:]
    one, two = moments(clip_of(total_ref) * grad_ref[...], first_ref[...], second_ref[...])
    clip_other = clip_other_ref[0, :1, :1].astype(F32) + clip_other_ref[1, :1, :1].astype(F32)
    scaled_other = clip_other * grad_other_ref[...].astype(F32)
    one_other, two_other = moments(scaled_other, first_other_ref[...], second_other_ref[...])
    w_ref[...] = mean(stepped(old_ref[...], one, two), stepped(old_other_ref[...], one_other, two_other))
    one_ref[...] = mean(one, one_other)
    two_ref[...] = mean(two, two_other)


STEP_ROWS = 512
TOTAL = pl.BlockSpec((8, 128), lambda i: (0, 0))


def columns(width, at=0):
    return pl.BlockSpec((STEP_ROWS, width), lambda i: (i, at // width))


def pair_of(width):
    return pl.BlockSpec((2, STEP_ROWS, width), lambda i: (0, i, 0))


def cost(rows, width, flops, size):
    return pl.CostEstimate(flops=flops * rows * width, bytes_accessed=size * rows * width, transcendentals=0)


def make(total, grad, within, first, second, old, at, width):
    rows = grad.shape[0]
    wide = columns(width, at)
    return pl.pallas_call(
        make_kernel,
        grid=(rows // STEP_ROWS,),
        out_shape=(jax.ShapeDtypeStruct((2, rows, width), BF16), jax.ShapeDtypeStruct((rows, width), BF16)),
        in_specs=[TOTAL, columns(width, within), wide, wide, wide],
        out_specs=(pair_of(width), columns(width)),
        cost_estimate=cost(rows, width, 30, 16),
    )(total, grad, first, second, old)


def mix(pair, step, pair_other, old_other, at, width, shape, outs):
    rows = shape[0]
    depth = rows if width == 128 else STEP_ROWS
    wide = pl.BlockSpec((depth, width), lambda i: (i, at // width))
    whole = jax.ShapeDtypeStruct(shape, BF16)
    return pl.pallas_call(
        mix_kernel,
        grid=(rows // depth,),
        out_shape=(whole, whole, whole, jax.ShapeDtypeStruct((8, 128), F32)),
        in_specs=[
            pl.BlockSpec((2, depth, width), lambda i: (0, i, 0)),
            pl.BlockSpec((depth, width), lambda i: (i, 0)),
            pl.BlockSpec(memory_space=pltpu.VMEM),
            wide,
        ]
        + [ANYWHERE] * len(outs),
        out_specs=(wide, wide, wide, TOTAL),
        input_output_aliases={4 + i: i for i in range(len(outs))},
        cost_estimate=cost(rows, width, 30, 18),
    )(pair, step, pair_other, old_other, *outs)


def early(total, pair_other, grad, grad_other, first, second, other, old, old_other, width, outs):
    rows, cols = old.shape
    wide = columns(width)
    shape = jax.ShapeDtypeStruct((rows, cols), BF16)
    return pl.pallas_call(
        early_kernel,
        grid=(rows // STEP_ROWS,),
        out_shape=(shape, shape, shape),
        in_specs=[TOTAL, pl.BlockSpec((2, 16, 128), lambda i: (0, rows // 16, 0))] + [wide] * 5 + [columns(width, width), wide, wide] + [ANYWHERE] * 3,
        out_specs=(wide, wide, wide),
        input_output_aliases={10 + i: i for i in range(3)},
        cost_estimate=cost(rows, width, 60, 22),
    )(total, pair_other, grad, grad_other, first, second, other, other, old, old_other, *outs)


def times(x, u):
    return lax.dot_general(x, u, (((0,), (0,)), ((), ())), preferred_element_type=F32)


def local_kernel(x_ref, u_ref, out_ref):
    out_ref[...] = times(x_ref[0], u_ref[...])


def local_product(x, u):
    blocks, depth, step = x.shape
    width = u.shape[1]
    return pl.pallas_call(
        local_kernel,
        grid=(blocks // 2,),
        out_shape=jax.ShapeDtypeStruct((blocks // 2 * step, width), F32),
        in_specs=[pl.BlockSpec((1, depth, step), lambda i: (i, 0, 0)), pl.BlockSpec((depth, width), lambda i: (0, 0))],
        out_specs=pl.BlockSpec((step, width), lambda i: (i, 0)),
        cost_estimate=SLIGHT,
        compiler_params=pltpu.CompilerParams(vmem_limit_bytes=32 * 2**20),
    )(x, u)


def finish_kernel(x_ref, u_ref, local_ref, *rest):
    grad_ref, squares_ref = rest[-2:]
    grad = local_ref[...] + times(x_ref[0], u_ref[...])
    grad_ref[...] = grad
    square = grad * grad
    lanes = sum(square[:, k : k + 128] for k in range(0, grad.shape[1], 128))

    @pl.when(pl.program_id(0) == 0)
    def _():
        squares_ref[...] = jnp.zeros_like(squares_ref)

    squares_ref[...] += jnp.sum(lanes.reshape(-1, 8, 128), axis=0)


def finish(x, u, local, earlier):
    blocks, depth, step = x.shape
    width = u.shape[1]
    rows = pl.BlockSpec((step, width), lambda i: (i, 0))
    return pl.pallas_call(
        finish_kernel,
        grid=(blocks // 2,),
        out_shape=(jax.ShapeDtypeStruct((blocks // 2 * step, width), F32), jax.ShapeDtypeStruct((8, 128), F32)),
        in_specs=[pl.BlockSpec((1, depth, step), lambda i: (blocks // 2 + i, 0, 0)), pl.BlockSpec((depth, width), lambda i: (0, 0)), rows] + [corner(value) for value in earlier],
        out_specs=(rows, pl.BlockSpec((8, 128), lambda i: (0, 0))),
        cost_estimate=SLIGHT,
        compiler_params=pltpu.CompilerParams(vmem_limit_bytes=32 * 2**20),
    )(x, u, local, *earlier)


EARLY = 256
UP = ((0, 768), (768, 768), (1536, 256))
LATE = ((256, 256), (512, 256), (768, 384), (1152, 384), (1536, 128), (1664, 128))


def part(value, piece):
    return value[:, piece[0] : piece[0] + piece[1]]


def holder(pieces, at):
    index = next(i for i, (start, width) in enumerate(pieces) if start <= at < start + width)
    return index, at - pieces[index][0]


def body(tokens, grad_out, weights, first_moment, second_moment):
    upstream, old = grad_out[0], weights[0]
    first, second = first_moment[0], second_moment[0]

    settled = settle(tokens[0])
    up = [part(upstream, piece) for piece in UP]
    up_other = [swap_dp(piece) for piece in up]
    old_other = across(old)
    state_other = across(jnp.concatenate([first[:, :EARLY], second[:, :EARLY]], axis=1))

    (near,) = gate((along_y(settled),), (up_other[0],))
    features = assemble(near, turned(near[:2], 1), turned(near[2:], 1))
    grads, squares = [], jnp.zeros((8, 128), F32)
    for i, (piece, other) in enumerate(zip(up, up_other)):
        grad, square = finish(features, other, local_product(features, piece), (old_other,) if i == 2 else ())
        grads.append(grad)
        squares = squares + square
    grad_other = across(grads[0][:, :EARLY].astype(BF16))
    total = group_sum(squares, (state_other,))

    pairs, steps, received, flags = [], [], [], []
    outs = ()
    for i in range(len(LATE) + 2):
        if i < len(LATE):
            at, width = LATE[i]
            chunk, within = holder(UP, at)
            build = make if i else make_first
            pair, step = build(total, grads[chunk], within, first, second, old, at, width)
            if i == 0:
                (pair,) = gate((pair,), (grad_other,))
            elif i > 1:
                (pair,) = gate((pair,), (received[i - 2],) + ((flags[i - 3],) if i > 2 else ()))
            pairs.append(pair)
            steps.append(step)
            received.append(across(pair))
        if i >= 2:
            j = i - 2
            at, width = LATE[j]
            *outs, flag = mix(pairs[j], steps[j], received[j], old_other, at, width, old.shape, outs)
            flags.append(flag)
        if i == 3:
            outs = early(total, received[0], grads[0], grad_other, first, second, state_other, old, old_other, EARLY, outs)
    return tuple(out[None] for out in outs)


def solution(mesh):
    placed = P("replica", "dp", "tensor")
    return jax.shard_map(
        body,
        mesh=mesh,
        in_specs=(placed,) * 5,
        out_specs=(placed,) * 3,
        check_vma=False,
    )
```

```python
import functools

import jax
import jax.numpy as jnp
from jax import lax
from jax.experimental import pallas as pl
from jax.experimental.pallas import tpu as pltpu
from jax.sharding import PartitionSpec as P

D = 2048
FF = 14336
STEP = 1
FIX_ONE = 1.0 - 0.9**STEP
FIX_TWO = 1.0 - 0.95**STEP
BF16 = jnp.bfloat16
ANYWHERE = pl.BlockSpec(memory_space=pl.ANY)
SLIGHT = pl.CostEstimate(flops=0, bytes_accessed=4096, transcendentals=0)
F32 = jnp.float32


def across(value):
    return lax.ppermute(value, "replica", [(s, s ^ 4) for s in range(8)])


def swap_dp(value):
    return lax.ppermute(value, "dp", [(0, 1), (1, 0)])


def nothing_kernel(*refs):
    del refs


def corner(value):
    if value.ndim > 2:
        return pl.BlockSpec(memory_space=pltpu.VMEM)
    return pl.BlockSpec((1,) * (value.ndim - 2) + (16 if value.dtype == BF16 else 8, 128), lambda i: (0,) * value.ndim)


def gate(values, earlier, size=4096):
    return pl.pallas_call(
        nothing_kernel,
        grid=(1,),
        out_shape=[jax.ShapeDtypeStruct(value.shape, value.dtype) for value in values],
        in_specs=[ANYWHERE] * len(values) + [corner(value) for value in earlier],
        out_specs=[ANYWHERE] * len(values),
        input_output_aliases={i: i for i in range(len(values))},
        cost_estimate=pl.CostEstimate(flops=0, bytes_accessed=size, transcendentals=0),
        compiler_params=pltpu.CompilerParams(vmem_limit_bytes=4 * 2**20),
    )(*values, *earlier)


def turned(value, bits):
    return lax.ppermute(value, "tensor", [(t, t ^ bits) for t in range(8)])


def settle(mine):
    pairs = []
    for d in range(2):
        for t in range(8):
            stays = t // 4 == d
            pairs.append((d * 8 + t, d * 8 + t if stays else (1 - d) * 8 + (t ^ 6)))
    return lax.ppermute(mine, ("dp", "tensor"), pairs)


def along_y(value):
    copies = jnp.broadcast_to(value, (4, *value.shape))
    return lax.all_to_all(copies, "tensor", 0, 0, tiled=True, axis_index_groups=[[0, 2, 4, 6], [1, 3, 5, 7]])


def assemble_kernel(slot_ref, near_ref, low_ref, high_ref, out_ref):
    for k in range(4):
        out_ref[slot_ref[k]] = near_ref[k]
    for k in range(2):
        out_ref[slot_ref[4 + k]] = low_ref[k]
        out_ref[slot_ref[6 + k]] = high_ref[k]


def assemble(near, low, high):
    core = lax.axis_index("tensor") % 2
    flip = 4 * lax.axis_index("dp")
    places = jnp.stack([(2 * y + core) ^ flip for y in range(4)] + [(2 * y + 1 - core) ^ flip for y in range(4)])
    slots = places ^ (places // 4 * 2)
    whole = pl.BlockSpec(memory_space=pltpu.VMEM)
    return pl.pallas_call(
        assemble_kernel,
        out_shape=jax.ShapeDtypeStruct((8, *near.shape[1:]), BF16),
        in_specs=[pl.BlockSpec(memory_space=pltpu.SMEM)] + [whole] * 3,
        out_specs=whole,
        cost_estimate=SLIGHT,
        compiler_params=pltpu.CompilerParams(vmem_limit_bytes=24 * 2**20),
    )(slots.astype(jnp.int32), near, low, high)


def add_kernel(one_ref, two_ref, *rest):
    rest[-1][...] = one_ref[...] + two_ref[...]


def group_sum(value, earlier):
    value = value + turned(value, 1)
    value = value + turned(value, 2) + turned(value, 4) + turned(value, 6)
    return pl.pallas_call(
        add_kernel,
        grid=(1,),
        out_shape=jax.ShapeDtypeStruct(value.shape, F32),
        in_specs=[corner(value)] * 2 + [corner(item) for item in earlier],
        out_specs=corner(value),
        cost_estimate=SLIGHT,
        compiler_params=pltpu.CompilerParams(vmem_limit_bytes=4 * 2**20),
    )(value, swap_dp(value), *earlier)


def clip_of(total_ref):
    total = jnp.sum(total_ref[...], keepdims=True)
    return jnp.minimum(1.0, 1.0 / jnp.sqrt(total / (D * FF) + 1e-06))


def moments(scaled, first, second):
    one = 0.9 * first.astype(F32) + 0.1 * scaled
    two = 0.95 * second.astype(F32) + 0.05 * scaled * scaled
    return one.astype(BF16), two.astype(BF16)


def stepped(old, one, two):
    old = old.astype(F32)
    update = (one.astype(F32) * (1.0 / FIX_ONE)) / (jnp.sqrt(two.astype(F32) * (1.0 / FIX_TWO)) + 1e-08)
    return (old - 0.05 * (update + 0.1 * old)).astype(BF16)


def mean(a, b):
    return (0.5 * (a.astype(F32) + b.astype(F32))).astype(BF16)


def make_kernel(total_ref, grad_ref, first_ref, second_ref, old_ref, pair_ref, step_ref):
    one, two = moments(clip_of(total_ref) * grad_ref[...], first_ref[...], second_ref[...])
    pair_ref[0] = one
    pair_ref[1] = two
    step_ref[...] = stepped(old_ref[...], one, two)


def make_first_kernel(total_ref, grad_ref, first_ref, second_ref, pair_ref):
    rows = grad_ref.shape[0]
    clip = clip_of(total_ref)
    one, two = moments(clip * grad_ref[...], first_ref[...], second_ref[...])
    pair_ref[0, :rows] = one
    pair_ref[1, :rows] = two
    clip = jnp.broadcast_to(clip, (16, grad_ref.shape[1]))
    high = clip.astype(BF16)
    pair_ref[0, rows:] = high
    pair_ref[1, rows:] = (clip - high.astype(F32)).astype(BF16)


def make_first(total, grad, within, first, second):
    rows, width = first.shape
    chosen = lambda start: pl.BlockSpec((rows, width), lambda i: (0, start // width))
    return pl.pallas_call(
        make_first_kernel,
        grid=(1,),
        out_shape=jax.ShapeDtypeStruct((2, rows + 16, width), BF16),
        in_specs=[TOTAL, chosen(within), chosen(0), chosen(0)],
        out_specs=pl.BlockSpec((2, rows + 16, width), lambda i: (0, 0, 0)),
        cost_estimate=cost(rows, width, 30, 16),
        compiler_params=pltpu.CompilerParams(vmem_limit_bytes=24 * 2**20),
    )(total, grad, first, second)


def mix_kernel(ready, pair_ref, step_ref, pair_other_ref, old_other_ref, *rest):
    w_ref, one_ref, two_ref, flag_ref = rest[-4:]
    flag_ref[...] = jnp.zeros_like(flag_ref)
    depth = step_ref.shape[0]
    here = pl.ds(pl.multiple_of(pl.program_id(0) * depth, depth), depth)
    one_other, two_other = pair_other_ref[0, here], pair_other_ref[1, here]
    step = step_ref[...] if ready else stepped(step_ref[...], pair_ref[0], pair_ref[1])
    w_ref[...] = mean(step, stepped(old_other_ref[...], one_other, two_other))
    one_ref[...] = mean(pair_ref[0], one_other)
    two_ref[...] = mean(pair_ref[1], two_other)


def early_kernel(
    total_ref,
    clip_other_ref,
    grad_ref,
    grad_other_ref,
    first_ref,
    second_ref,
    first_other_ref,
    second_other_ref,
    old_ref,
    old_other_ref,
    *rest,
):
    w_ref, one_ref, two_ref = rest[-3:]
    one, two = moments(clip_of(total_ref) * grad_ref[...], first_ref[...], second_ref[...])
    clip_other = clip_other_ref[0, :1, :1].astype(F32) + clip_other_ref[1, :1, :1].astype(F32)
    scaled_other = clip_other * grad_other_ref[...].astype(F32)
    one_other, two_other = moments(scaled_other, first_other_ref[...], second_other_ref[...])
    w_ref[...] = mean(stepped(old_ref[...], one, two), stepped(old_other_ref[...], one_other, two_other))
    one_ref[...] = mean(one, one_other)
    two_ref[...] = mean(two, two_other)


STEP_ROWS = 512
TOTAL = pl.BlockSpec((8, 128), lambda i: (0, 0))


def columns(width, at=0):
    return pl.BlockSpec((STEP_ROWS, width), lambda i: (i, at // width))


def pair_of(width):
    return pl.BlockSpec((2, STEP_ROWS, width), lambda i: (0, i, 0))


def cost(rows, width, flops, size):
    return pl.CostEstimate(flops=flops * rows * width, bytes_accessed=size * rows * width, transcendentals=0)


def make(total, grad, within, first, second, old, at, width):
    rows = grad.shape[0]
    wide = columns(width, at)
    return pl.pallas_call(
        make_kernel,
        grid=(rows // STEP_ROWS,),
        out_shape=(jax.ShapeDtypeStruct((2, rows, width), BF16), jax.ShapeDtypeStruct((rows, width), BF16)),
        in_specs=[TOTAL, columns(width, within), wide, wide, wide],
        out_specs=(pair_of(width), columns(width)),
        cost_estimate=cost(rows, width, 30, 16),
    )(total, grad, first, second, old)


def mix(pair, step, ready, pair_other, old_other, at, width, shape, outs):
    rows = shape[0]
    depth = rows if width == 128 else STEP_ROWS
    wide = pl.BlockSpec((depth, width), lambda i: (i, at // width))
    whole = jax.ShapeDtypeStruct(shape, BF16)
    return pl.pallas_call(
        functools.partial(mix_kernel, ready),
        grid=(rows // depth,),
        out_shape=(whole, whole, whole, jax.ShapeDtypeStruct((8, 128), F32)),
        in_specs=[
            pl.BlockSpec((2, depth, width), lambda i: (0, i, 0)),
            pl.BlockSpec((depth, width), lambda i: (i, 0)),
            pl.BlockSpec(memory_space=pltpu.VMEM),
            wide,
        ]
        + [ANYWHERE] * len(outs),
        out_specs=(wide, wide, wide, TOTAL),
        input_output_aliases={4 + i: i for i in range(len(outs))},
        cost_estimate=cost(rows, width, 30, 18),
        compiler_params=pltpu.CompilerParams(vmem_limit_bytes=16 * 2**20),
    )(pair, step, pair_other, old_other, *outs)


def early(total, pair_other, grad, grad_other, first, second, other, old, old_other, width, outs):
    rows, cols = old.shape
    wide = columns(width)
    shape = jax.ShapeDtypeStruct((rows, cols), BF16)
    return pl.pallas_call(
        early_kernel,
        grid=(rows // STEP_ROWS,),
        out_shape=(shape, shape, shape),
        in_specs=[TOTAL, pl.BlockSpec((2, 16, 128), lambda i: (0, rows // 16, 0))] + [wide] * 5 + [columns(width, width), wide, wide] + [ANYWHERE] * 3,
        out_specs=(wide, wide, wide),
        input_output_aliases={10 + i: i for i in range(3)},
        cost_estimate=cost(rows, width, 60, 22),
    )(total, pair_other, grad, grad_other, first, second, other, other, old, old_other, *outs)


def times(x, u):
    return lax.dot_general(x, u, (((0,), (0,)), ((), ())), preferred_element_type=F32)


def local_kernel(x_ref, u_ref, out_ref):
    out_ref[...] = times(x_ref[0], u_ref[...])


def local_product(x, u):
    blocks, depth, step = x.shape
    width = u.shape[1]
    return pl.pallas_call(
        local_kernel,
        grid=(blocks // 2,),
        out_shape=jax.ShapeDtypeStruct((blocks // 2 * step, width), F32),
        in_specs=[pl.BlockSpec((1, depth, step), lambda i: (i, 0, 0)), pl.BlockSpec((depth, width), lambda i: (0, 0))],
        out_specs=pl.BlockSpec((step, width), lambda i: (i, 0)),
        cost_estimate=SLIGHT,
        compiler_params=pltpu.CompilerParams(vmem_limit_bytes=32 * 2**20),
    )(x, u)


def finish_kernel(x_ref, u_ref, local_ref, *rest):
    grad_ref, squares_ref = rest[-2:]
    grad = local_ref[...] + times(x_ref[0], u_ref[...])
    grad_ref[...] = grad
    square = grad * grad
    lanes = sum(square[:, k : k + 128] for k in range(0, grad.shape[1], 128))

    @pl.when(pl.program_id(0) == 0)
    def _():
        squares_ref[...] = jnp.zeros_like(squares_ref)

    squares_ref[...] += jnp.sum(lanes.reshape(-1, 8, 128), axis=0)


def finish(x, u, local, earlier):
    blocks, depth, step = x.shape
    width = u.shape[1]
    rows = pl.BlockSpec((step, width), lambda i: (i, 0))
    return pl.pallas_call(
        finish_kernel,
        grid=(blocks // 2,),
        out_shape=(jax.ShapeDtypeStruct((blocks // 2 * step, width), F32), jax.ShapeDtypeStruct((8, 128), F32)),
        in_specs=[pl.BlockSpec((1, depth, step), lambda i: (blocks // 2 + i, 0, 0)), pl.BlockSpec((depth, width), lambda i: (0, 0)), rows] + [corner(value) for value in earlier],
        out_specs=(rows, pl.BlockSpec((8, 128), lambda i: (0, 0))),
        cost_estimate=SLIGHT,
        compiler_params=pltpu.CompilerParams(vmem_limit_bytes=32 * 2**20),
    )(x, u, local, *earlier)


EARLY = 256
UP = ((0, 768), (768, 768), (1536, 256))
LATE = ((256, 256), (512, 256), (768, 384), (1152, 384), (1536, 128), (1664, 128))


def part(value, piece):
    return value[:, piece[0] : piece[0] + piece[1]]


def holder(pieces, at):
    index = next(i for i, (start, width) in enumerate(pieces) if start <= at < start + width)
    return index, at - pieces[index][0]


def body(tokens, grad_out, weights, first_moment, second_moment):
    upstream, old = grad_out[0], weights[0]
    first, second = first_moment[0], second_moment[0]

    settled = settle(tokens[0])
    up = [part(upstream, piece) for piece in UP]
    up_other = [swap_dp(piece) for piece in up]
    old_other = across(old)
    state_other = across(jnp.concatenate([first[:, :EARLY], second[:, :EARLY]], axis=1))

    near, *leading = gate((along_y(settled), *(part(value, LATE[0]) for value in (first, second))), (up_other[0],))
    features = assemble(near, turned(near[:2], 1), turned(near[2:], 1))
    grads, squares = [], jnp.zeros((8, 128), F32)
    for i, (piece, other) in enumerate(zip(up, up_other)):
        grad, square = finish(features, other, local_product(features, piece), (old_other,) if i == 2 else ())
        grads.append(grad)
        squares = squares + square
    grad_other = across(grads[0][:, :EARLY].astype(BF16))
    total = group_sum(squares, (state_other,))

    pairs, steps, received, flags = [], [], [], []
    outs = ()
    for i in range(len(LATE) + 2):
        if i < len(LATE):
            at, width = LATE[i]
            chunk, within = holder(UP, at)
            if i:
                pair, step = make(total, grads[chunk], within, first, second, old, at, width)
            else:
                pair, step = make_first(total, grads[chunk], within, *leading), part(old, LATE[0])
            if i == 0:
                (pair,) = gate((pair,), (grad_other,))
            elif i > 1:
                (pair,) = gate((pair,), (received[i - 2],) + ((flags[i - 3],) if i > 2 else ()))
            pairs.append(pair)
            steps.append(step)
            received.append(across(pair))
        if i >= 2:
            j = i - 2
            at, width = LATE[j]
            *outs, flag = mix(pairs[j], steps[j], j > 0, received[j], old_other, at, width, old.shape, outs)
            flags.append(flag)
        if i == 3:
            outs = early(total, received[0], grads[0], grad_other, first, second, state_other, old, old_other, EARLY, outs)
    return tuple(out[None] for out in outs)


def solution(mesh):
    placed = P("replica", "dp", "tensor")
    return jax.shard_map(
        body,
        mesh=mesh,
        in_specs=(placed,) * 5,
        out_specs=(placed,) * 3,
        check_vma=False,
    )
```

```python
import functools

import jax
import jax.numpy as jnp
from jax import lax
from jax.experimental import pallas as pl
from jax.experimental.pallas import tpu as pltpu
from jax.sharding import PartitionSpec as P

D = 2048
FF = 14336
STEP = 1
FIX_ONE = 1.0 - 0.9**STEP
FIX_TWO = 1.0 - 0.95**STEP
BF16 = jnp.bfloat16
ANYWHERE = pl.BlockSpec(memory_space=pl.ANY)
SLIGHT = pl.CostEstimate(flops=0, bytes_accessed=4096, transcendentals=0)
F32 = jnp.float32


def across(value):
    return lax.ppermute(value, "replica", [(s, s ^ 4) for s in range(8)])


def swap_dp(value):
    return lax.ppermute(value, "dp", [(0, 1), (1, 0)])


def nothing_kernel(*refs):
    del refs


def corner(value):
    if value.ndim > 2:
        return pl.BlockSpec(memory_space=pltpu.VMEM)
    return pl.BlockSpec((1,) * (value.ndim - 2) + (16 if value.dtype == BF16 else 8, 128), lambda i: (0,) * value.ndim)


def gate(values, earlier, size=4096):
    return pl.pallas_call(
        nothing_kernel,
        grid=(1,),
        out_shape=[jax.ShapeDtypeStruct(value.shape, value.dtype) for value in values],
        in_specs=[ANYWHERE] * len(values) + [corner(value) for value in earlier],
        out_specs=[ANYWHERE] * len(values),
        input_output_aliases={i: i for i in range(len(values))},
        cost_estimate=pl.CostEstimate(flops=0, bytes_accessed=size, transcendentals=0),
        compiler_params=pltpu.CompilerParams(vmem_limit_bytes=4 * 2**20),
    )(*values, *earlier)


def turned(value, bits):
    return lax.ppermute(value, "tensor", [(t, t ^ bits) for t in range(8)])


def settle(mine):
    pairs = []
    for d in range(2):
        for t in range(8):
            stays = t // 4 == d
            pairs.append((d * 8 + t, d * 8 + t if stays else (1 - d) * 8 + (t ^ 6)))
    return lax.ppermute(mine, ("dp", "tensor"), pairs)


def along_y(value):
    copies = jnp.broadcast_to(value, (4, *value.shape))
    return lax.all_to_all(copies, "tensor", 0, 0, tiled=True, axis_index_groups=[[0, 2, 4, 6], [1, 3, 5, 7]])


def assemble_kernel(slot_ref, near_ref, low_ref, high_ref, out_ref):
    for k in range(4):
        out_ref[slot_ref[k]] = near_ref[k]
    for k in range(2):
        out_ref[slot_ref[4 + k]] = low_ref[k]
        out_ref[slot_ref[6 + k]] = high_ref[k]


def assemble(near, low, high):
    core = lax.axis_index("tensor") % 2
    flip = 4 * lax.axis_index("dp")
    places = jnp.stack([(2 * y + core) ^ flip for y in range(4)] + [(2 * y + 1 - core) ^ flip for y in range(4)])
    slots = places ^ (places // 4 * 2)
    whole = pl.BlockSpec(memory_space=pltpu.VMEM)
    return pl.pallas_call(
        assemble_kernel,
        out_shape=jax.ShapeDtypeStruct((8, *near.shape[1:]), BF16),
        in_specs=[pl.BlockSpec(memory_space=pltpu.SMEM)] + [whole] * 3,
        out_specs=whole,
        cost_estimate=SLIGHT,
        compiler_params=pltpu.CompilerParams(vmem_limit_bytes=24 * 2**20),
    )(slots.astype(jnp.int32), near, low, high)


def add_kernel(one_ref, two_ref, *rest):
    rest[-1][...] = one_ref[...] + two_ref[...]


def group_sum(value, earlier):
    value = value + turned(value, 1)
    value = value + turned(value, 2) + turned(value, 4) + turned(value, 6)
    return pl.pallas_call(
        add_kernel,
        grid=(1,),
        out_shape=jax.ShapeDtypeStruct(value.shape, F32),
        in_specs=[corner(value)] * 2 + [corner(item) for item in earlier],
        out_specs=corner(value),
        cost_estimate=SLIGHT,
        compiler_params=pltpu.CompilerParams(vmem_limit_bytes=4 * 2**20),
    )(value, swap_dp(value), *earlier)


def clip_of(total_ref):
    total = jnp.sum(total_ref[...], keepdims=True)
    return jnp.minimum(1.0, 1.0 / jnp.sqrt(total / (D * FF) + 1e-06))


def moments(scaled, first, second):
    one = 0.9 * first.astype(F32) + 0.1 * scaled
    two = 0.95 * second.astype(F32) + 0.05 * scaled * scaled
    return one.astype(BF16), two.astype(BF16)


def stepped(old, one, two):
    old = old.astype(F32)
    update = (one.astype(F32) * (1.0 / FIX_ONE)) / (jnp.sqrt(two.astype(F32) * (1.0 / FIX_TWO)) + 1e-08)
    return (old - 0.05 * (update + 0.1 * old)).astype(BF16)


def mean(a, b):
    return (0.5 * (a.astype(F32) + b.astype(F32))).astype(BF16)


def make_kernel(total_ref, grad_ref, first_ref, second_ref, old_ref, pair_ref, step_ref):
    one, two = moments(clip_of(total_ref) * grad_ref[...], first_ref[...], second_ref[...])
    pair_ref[0] = one
    pair_ref[1] = two
    step_ref[...] = stepped(old_ref[...], one, two)


def make_first_kernel(total_ref, grad_ref, first_ref, second_ref, pair_ref):
    rows = grad_ref.shape[0]
    clip = clip_of(total_ref)
    one, two = moments(clip * grad_ref[...], first_ref[...], second_ref[...])
    pair_ref[0, :rows] = one
    pair_ref[1, :rows] = two
    clip = jnp.broadcast_to(clip, (16, grad_ref.shape[1]))
    high = clip.astype(BF16)
    pair_ref[0, rows:] = high
    pair_ref[1, rows:] = (clip - high.astype(F32)).astype(BF16)


def make_first(total, grad, within, first, second):
    rows, width = first.shape
    chosen = lambda start: pl.BlockSpec((rows, width), lambda i: (0, start // width))
    return pl.pallas_call(
        make_first_kernel,
        grid=(1,),
        out_shape=jax.ShapeDtypeStruct((2, rows + 16, width), BF16),
        in_specs=[TOTAL, chosen(within), chosen(0), chosen(0)],
        out_specs=pl.BlockSpec((2, rows + 16, width), lambda i: (0, 0, 0)),
        cost_estimate=cost(rows, width, 30, 16),
        compiler_params=pltpu.CompilerParams(vmem_limit_bytes=24 * 2**20),
    )(total, grad, first, second)


def mix_kernel(ready, pair_ref, step_ref, pair_other_ref, old_other_ref, *rest):
    w_ref, one_ref, two_ref, flag_ref = rest[-4:]
    flag_ref[...] = jnp.zeros_like(flag_ref)
    depth = step_ref.shape[0]
    here = pl.ds(pl.multiple_of(pl.program_id(0) * depth, depth), depth)
    one_other, two_other = pair_other_ref[0, here], pair_other_ref[1, here]
    step = step_ref[...] if ready else stepped(step_ref[...], pair_ref[0], pair_ref[1])
    w_ref[...] = mean(step, stepped(old_other_ref[...], one_other, two_other))
    one_ref[...] = mean(pair_ref[0], one_other)
    two_ref[...] = mean(pair_ref[1], two_other)


def early_kernel(
    total_ref,
    clip_other_ref,
    grad_ref,
    grad_other_ref,
    first_ref,
    second_ref,
    first_other_ref,
    second_other_ref,
    second_rest_ref,
    old_ref,
    old_other_ref,
    *rest,
):
    w_ref, one_ref, two_ref = rest[-3:]
    one, two = moments(clip_of(total_ref) * grad_ref[...], first_ref[...], second_ref[...])
    second_other = jnp.concatenate([second_other_ref[...], second_rest_ref[...]], axis=1)
    clip_other = clip_other_ref[0, :1, :1].astype(F32) + clip_other_ref[1, :1, :1].astype(F32)
    scaled_other = clip_other * grad_other_ref[...].astype(F32)
    one_other, two_other = moments(scaled_other, first_other_ref[...], second_other)
    w_ref[...] = mean(stepped(old_ref[...], one, two), stepped(old_other_ref[...], one_other, two_other))
    one_ref[...] = mean(one, one_other)
    two_ref[...] = mean(two, two_other)


STEP_ROWS = 512
TOTAL = pl.BlockSpec((8, 128), lambda i: (0, 0))


def columns(width, at=0):
    return pl.BlockSpec((STEP_ROWS, width), lambda i: (i, at // width))


def pair_of(width):
    return pl.BlockSpec((2, STEP_ROWS, width), lambda i: (0, i, 0))


def cost(rows, width, flops, size):
    return pl.CostEstimate(flops=flops * rows * width, bytes_accessed=size * rows * width, transcendentals=0)


def make(total, grad, within, first, second, old, at, width):
    rows = grad.shape[0]
    wide = columns(width, at)
    return pl.pallas_call(
        make_kernel,
        grid=(rows // STEP_ROWS,),
        out_shape=(jax.ShapeDtypeStruct((2, rows, width), BF16), jax.ShapeDtypeStruct((rows, width), BF16)),
        in_specs=[TOTAL, columns(width, within), wide, wide, wide],
        out_specs=(pair_of(width), columns(width)),
        cost_estimate=cost(rows, width, 30, 16),
    )(total, grad, first, second, old)


def mix(pair, step, ready, pair_other, old_other, at, width, shape, outs):
    rows = shape[0]
    depth = rows if width == 128 else STEP_ROWS
    wide = pl.BlockSpec((depth, width), lambda i: (i, at // width))
    whole = jax.ShapeDtypeStruct(shape, BF16)
    return pl.pallas_call(
        functools.partial(mix_kernel, ready),
        grid=(rows // depth,),
        out_shape=(whole, whole, whole, jax.ShapeDtypeStruct((8, 128), F32)),
        in_specs=[
            pl.BlockSpec((2, depth, width), lambda i: (0, i, 0)),
            pl.BlockSpec((depth, width), lambda i: (i, 0)),
            pl.BlockSpec(memory_space=pltpu.VMEM),
            wide,
        ]
        + [ANYWHERE] * len(outs),
        out_specs=(wide, wide, wide, TOTAL),
        input_output_aliases={4 + i: i for i in range(len(outs))},
        cost_estimate=cost(rows, width, 30, 18),
        compiler_params=pltpu.CompilerParams(vmem_limit_bytes=16 * 2**20),
    )(pair, step, pair_other, old_other, *outs)


def early(total, pair_other, grad, grad_other, first, second, other, old, old_other, width, outs):
    rows, cols = old.shape
    wide = columns(width)
    shape = jax.ShapeDtypeStruct((rows, cols), BF16)
    return pl.pallas_call(
        early_kernel,
        grid=(rows // STEP_ROWS,),
        out_shape=(shape, shape, shape),
        in_specs=[TOTAL, pl.BlockSpec((2, 16, 128), lambda i: (0, rows // 16, 0))] + [wide] * 5 + [columns(width // 2, width)] * 2 + [wide, wide] + [ANYWHERE] * 3,
        out_specs=(wide, wide, wide),
        input_output_aliases={11 + i: i for i in range(3)},
        cost_estimate=cost(rows, width, 60, 22),
    )(total, pair_other, grad, grad_other, first, second, other, other, grad_other, old, old_other, *outs)


def times(x, u):
    return lax.dot_general(x, u, (((0,), (0,)), ((), ())), preferred_element_type=F32)


def local_kernel(x_ref, u_ref, out_ref):
    out_ref[...] = times(x_ref[0], u_ref[...])


def local_product(x, u):
    blocks, depth, step = x.shape
    width = u.shape[1]
    return pl.pallas_call(
        local_kernel,
        grid=(blocks // 2,),
        out_shape=jax.ShapeDtypeStruct((blocks // 2 * step, width), F32),
        in_specs=[pl.BlockSpec((1, depth, step), lambda i: (i, 0, 0)), pl.BlockSpec((depth, width), lambda i: (0, 0))],
        out_specs=pl.BlockSpec((step, width), lambda i: (i, 0)),
        cost_estimate=SLIGHT,
        compiler_params=pltpu.CompilerParams(vmem_limit_bytes=32 * 2**20),
    )(x, u)


def finish_kernel(x_ref, u_ref, local_ref, *rest):
    grad_ref, squares_ref = rest[-2:]
    grad = local_ref[...] + times(x_ref[0], u_ref[...])
    grad_ref[...] = grad
    square = grad * grad
    lanes = sum(square[:, k : k + 128] for k in range(0, grad.shape[1], 128))

    @pl.when(pl.program_id(0) == 0)
    def _():
        squares_ref[...] = jnp.zeros_like(squares_ref)

    squares_ref[...] += jnp.sum(lanes.reshape(-1, 8, 128), axis=0)


def finish(x, u, local, earlier):
    blocks, depth, step = x.shape
    width = u.shape[1]
    rows = pl.BlockSpec((step, width), lambda i: (i, 0))
    return pl.pallas_call(
        finish_kernel,
        grid=(blocks // 2,),
        out_shape=(jax.ShapeDtypeStruct((blocks // 2 * step, width), F32), jax.ShapeDtypeStruct((8, 128), F32)),
        in_specs=[pl.BlockSpec((1, depth, step), lambda i: (blocks // 2 + i, 0, 0)), pl.BlockSpec((depth, width), lambda i: (0, 0)), rows] + [corner(value) for value in earlier],
        out_specs=(rows, pl.BlockSpec((8, 128), lambda i: (0, 0))),
        cost_estimate=SLIGHT,
        compiler_params=pltpu.CompilerParams(vmem_limit_bytes=32 * 2**20),
    )(x, u, local, *earlier)


EARLY = 256
UP = ((0, 768), (768, 768), (1536, 256))
FIRST = 2
LATE = ((256, 128), (384, 128), (512, 256), (1536, 128), (768, 384), (1152, 384), (1664, 128))


def part(value, piece):
    return value[:, piece[0] : piece[0] + piece[1]]


def holder(pieces, at):
    index = next(i for i, (start, width) in enumerate(pieces) if start <= at < start + width)
    return index, at - pieces[index][0]


def body(tokens, grad_out, weights, first_moment, second_moment):
    upstream, old = grad_out[0], weights[0]
    first, second = first_moment[0], second_moment[0]

    settled = settle(tokens[0])
    up = [part(upstream, piece) for piece in UP]
    up_other = [swap_dp(piece) for piece in up]
    old_other = across(old)
    state_other = across(jnp.concatenate([first[:, :EARLY], second[:, : EARLY // 2]], axis=1))

    near, *leading = gate(
        (along_y(settled), part(first, LATE[FIRST]), part(second, LATE[FIRST])), (up_other[0],)
    )
    features = assemble(near, turned(near[:2], 1), turned(near[2:], 1))
    grads, squares = [], jnp.zeros((8, 128), F32)
    for i, (piece, other) in enumerate(zip(up, up_other)):
        grad, square = finish(features, other, local_product(features, piece), (old_other,) if i == 2 else ())
        grads.append(grad)
        squares = squares + square
    grad_other = across(jnp.concatenate([grads[0][:, :EARLY].astype(BF16), second[:, EARLY // 2 : EARLY]], axis=1))
    total = group_sum(squares, (state_other,))

    pairs, steps, received, flags = [], [], [], []
    outs = ()
    for i in range(len(LATE) + 2):
        if i < len(LATE):
            at, width = LATE[i]
            chunk, within = holder(UP, at)
            if i == FIRST:
                pair, step = make_first(total, grads[chunk], within, *leading), part(old, LATE[i])
            else:
                pair, step = make(total, grads[chunk], within, first, second, old, at, width)
            if i == 1:
                (pair,) = gate((pair,), (grad_other,))
            elif i > 3:
                earlier = [(received[0], received[1], flags[0]), (*received[2:4], *flags[1:2]), (*received[4:5], *flags[3:4])][i - 4]
                (pair,) = gate((pair,), earlier)
            pairs.append(pair)
            steps.append(step)
            received.append(across(pair))
        if i >= 2:
            j = i - 2
            at, width = LATE[j]
            *outs, flag = mix(pairs[j], steps[j], j != FIRST, received[j], old_other, at, width, old.shape, outs)
            flags.append(flag)
        if i == FIRST + 2:
            outs = early(total, received[FIRST], grads[0], grad_other, first, second, state_other, old, old_other, EARLY, outs)
    return tuple(out[None] for out in outs)


def solution(mesh):
    placed = P("replica", "dp", "tensor")
    return jax.shard_map(
        body,
        mesh=mesh,
        in_specs=(placed,) * 5,
        out_specs=(placed,) * 3,
        check_vma=False,
    )
```

```python
import functools

import jax
import jax.numpy as jnp
from jax import lax
from jax.experimental import pallas as pl
from jax.experimental.pallas import tpu as pltpu
from jax.sharding import PartitionSpec as P

D = 2048
FF = 14336
STEP = 1
FIX_ONE = 1.0 - 0.9**STEP
FIX_TWO = 1.0 - 0.95**STEP
BF16 = jnp.bfloat16
ANYWHERE = pl.BlockSpec(memory_space=pl.ANY)
SLIGHT = pl.CostEstimate(flops=0, bytes_accessed=4096, transcendentals=0)
F32 = jnp.float32


def across(value):
    return lax.ppermute(value, "replica", [(s, s ^ 4) for s in range(8)])


def swap_dp(value):
    return lax.ppermute(value, "dp", [(0, 1), (1, 0)])


def nothing_kernel(*refs):
    del refs


def corner(value):
    if value.ndim > 2:
        return pl.BlockSpec(memory_space=pltpu.VMEM)
    return pl.BlockSpec((1,) * (value.ndim - 2) + (16 if value.dtype == BF16 else 8, 128), lambda i: (0,) * value.ndim)


def gate(values, earlier, size=4096):
    return pl.pallas_call(
        nothing_kernel,
        grid=(1,),
        out_shape=[jax.ShapeDtypeStruct(value.shape, value.dtype) for value in values],
        in_specs=[ANYWHERE] * len(values) + [corner(value) for value in earlier],
        out_specs=[ANYWHERE] * len(values),
        input_output_aliases={i: i for i in range(len(values))},
        cost_estimate=pl.CostEstimate(flops=0, bytes_accessed=size, transcendentals=0),
        compiler_params=pltpu.CompilerParams(vmem_limit_bytes=4 * 2**20),
    )(*values, *earlier)


def turned(value, bits):
    return lax.ppermute(value, "tensor", [(t, t ^ bits) for t in range(8)])


def settle(mine):
    pairs = []
    for d in range(2):
        for t in range(8):
            stays = t // 4 == d
            pairs.append((d * 8 + t, d * 8 + t if stays else (1 - d) * 8 + (t ^ 6)))
    return lax.ppermute(mine, ("dp", "tensor"), pairs)


def along_y(value):
    copies = jnp.broadcast_to(value, (4, *value.shape))
    return lax.all_to_all(copies, "tensor", 0, 0, tiled=True, axis_index_groups=[[0, 2, 4, 6], [1, 3, 5, 7]])


def assemble_kernel(slot_ref, near_ref, low_ref, high_ref, out_ref):
    for k in range(4):
        out_ref[slot_ref[k]] = near_ref[k]
    for k in range(2):
        out_ref[slot_ref[4 + k]] = low_ref[k]
        out_ref[slot_ref[6 + k]] = high_ref[k]


def assemble(near, low, high):
    core = lax.axis_index("tensor") % 2
    flip = 4 * lax.axis_index("dp")
    places = jnp.stack([(2 * y + core) ^ flip for y in range(4)] + [(2 * y + 1 - core) ^ flip for y in range(4)])
    slots = places ^ (places // 4 * 2)
    whole = pl.BlockSpec(memory_space=pltpu.VMEM)
    return pl.pallas_call(
        assemble_kernel,
        out_shape=jax.ShapeDtypeStruct((8, *near.shape[1:]), BF16),
        in_specs=[pl.BlockSpec(memory_space=pltpu.SMEM)] + [whole] * 3,
        out_specs=whole,
        cost_estimate=SLIGHT,
        compiler_params=pltpu.CompilerParams(vmem_limit_bytes=24 * 2**20),
    )(slots.astype(jnp.int32), near, low, high)


def add_kernel(one_ref, two_ref, *rest):
    rest[-1][...] = one_ref[...] + two_ref[...]


def group_sum(value, earlier):
    value = value + turned(value, 1)
    value = value + turned(value, 2) + turned(value, 4) + turned(value, 6)
    return pl.pallas_call(
        add_kernel,
        grid=(1,),
        out_shape=jax.ShapeDtypeStruct(value.shape, F32),
        in_specs=[corner(value)] * 2 + [corner(item) for item in earlier],
        out_specs=corner(value),
        cost_estimate=SLIGHT,
        compiler_params=pltpu.CompilerParams(vmem_limit_bytes=4 * 2**20),
    )(value, swap_dp(value), *earlier)


def clip_of(total_ref):
    total = jnp.sum(total_ref[...], keepdims=True)
    return jnp.minimum(1.0, 1.0 / jnp.sqrt(total / (D * FF) + 1e-06))


def moments(scaled, first, second):
    one = 0.9 * first.astype(F32) + 0.1 * scaled
    two = 0.95 * second.astype(F32) + 0.05 * scaled * scaled
    return one.astype(BF16), two.astype(BF16)


def stepped(old, one, two):
    old = old.astype(F32)
    update = (one.astype(F32) * (1.0 / FIX_ONE)) / (jnp.sqrt(two.astype(F32) * (1.0 / FIX_TWO)) + 1e-08)
    return (old - 0.05 * (update + 0.1 * old)).astype(BF16)


def mean(a, b):
    return (0.5 * (a.astype(F32) + b.astype(F32))).astype(BF16)


def make_kernel(total_ref, grad_ref, first_ref, second_ref, old_ref, pair_ref, step_ref):
    one, two = moments(clip_of(total_ref) * grad_ref[...], first_ref[...], second_ref[...])
    pair_ref[0] = one
    pair_ref[1] = two
    step_ref[...] = stepped(old_ref[...], one, two)


def make_first_kernel(total_ref, grad_ref, first_ref, second_ref, pair_ref):
    rows = grad_ref.shape[0]
    clip = clip_of(total_ref)
    one, two = moments(clip * grad_ref[...], first_ref[...], second_ref[...])
    pair_ref[0, :rows] = one
    pair_ref[1, :rows] = two
    clip = jnp.broadcast_to(clip, (16, grad_ref.shape[1]))
    high = clip.astype(BF16)
    pair_ref[0, rows:] = high
    pair_ref[1, rows:] = (clip - high.astype(F32)).astype(BF16)


def make_first(total, grad, within, first, second):
    rows, width = first.shape
    chosen = lambda start: pl.BlockSpec((rows, width), lambda i: (0, start // width))
    return pl.pallas_call(
        make_first_kernel,
        grid=(1,),
        out_shape=jax.ShapeDtypeStruct((2, rows + 16, width), BF16),
        in_specs=[TOTAL, chosen(within), chosen(0), chosen(0)],
        out_specs=pl.BlockSpec((2, rows + 16, width), lambda i: (0, 0, 0)),
        cost_estimate=cost(rows, width, 30, 16),
        compiler_params=pltpu.CompilerParams(vmem_limit_bytes=24 * 2**20),
    )(total, grad, first, second)


def mix_kernel(ready, pair_ref, step_ref, pair_other_ref, old_other_ref, *rest):
    w_ref, one_ref, two_ref, flag_ref = rest[-4:]
    flag_ref[...] = jnp.zeros_like(flag_ref)
    depth = step_ref.shape[0]
    here = pl.ds(pl.multiple_of(pl.program_id(0) * depth, depth), depth)
    one_other, two_other = pair_other_ref[0, here], pair_other_ref[1, here]
    step = step_ref[...] if ready else stepped(step_ref[...], pair_ref[0], pair_ref[1])
    w_ref[...] = mean(step, stepped(old_other_ref[...], one_other, two_other))
    one_ref[...] = mean(pair_ref[0], one_other)
    two_ref[...] = mean(pair_ref[1], two_other)


def early_kernel(
    total_ref,
    clip_other_ref,
    grad_ref,
    grad_other_ref,
    first_ref,
    second_ref,
    first_other_ref,
    second_other_ref,
    second_rest_ref,
    old_ref,
    old_other_ref,
    *rest,
):
    w_ref, one_ref, two_ref = rest[-3:]
    one, two = moments(clip_of(total_ref) * grad_ref[...], first_ref[...], second_ref[...])
    second_other = jnp.concatenate([second_other_ref[...], second_rest_ref[...]], axis=1)
    clip_other = clip_other_ref[0, :1, :1].astype(F32) + clip_other_ref[1, :1, :1].astype(F32)
    scaled_other = clip_other * grad_other_ref[...].astype(F32)
    one_other, two_other = moments(scaled_other, first_other_ref[...], second_other)
    w_ref[...] = mean(stepped(old_ref[...], one, two), stepped(old_other_ref[...], one_other, two_other))
    one_ref[...] = mean(one, one_other)
    two_ref[...] = mean(two, two_other)


STEP_ROWS = 512
TOTAL = pl.BlockSpec((8, 128), lambda i: (0, 0))


def columns(width, at=0):
    return pl.BlockSpec((STEP_ROWS, width), lambda i: (i, at // width))


def pair_of(width):
    return pl.BlockSpec((2, STEP_ROWS, width), lambda i: (0, i, 0))


def cost(rows, width, flops, size):
    return pl.CostEstimate(flops=flops * rows * width, bytes_accessed=size * rows * width, transcendentals=0)


def make(total, grad, within, first, second, old, at, width):
    rows = grad.shape[0]
    wide = columns(width, at)
    return pl.pallas_call(
        make_kernel,
        grid=(rows // STEP_ROWS,),
        out_shape=(jax.ShapeDtypeStruct((2, rows, width), BF16), jax.ShapeDtypeStruct((rows, width), BF16)),
        in_specs=[TOTAL, columns(width, within), wide, wide, wide],
        out_specs=(pair_of(width), columns(width)),
        cost_estimate=cost(rows, width, 30, 16),
    )(total, grad, first, second, old)


def mix(pair, step, ready, pair_other, old_other, at, width, shape, outs):
    rows = shape[0]
    narrow = width == 128
    depth = rows if narrow else STEP_ROWS
    inside = pl.BlockSpec(memory_space=pltpu.VMEM)
    wide = pl.BlockSpec((depth, width), lambda i: (i, at // width))
    whole = jax.ShapeDtypeStruct(shape, BF16)
    return pl.pallas_call(
        functools.partial(mix_kernel, ready),
        grid=(rows // depth,),
        out_shape=(whole, whole, whole, jax.ShapeDtypeStruct((8, 128), F32)),
        in_specs=[
            inside if narrow else pl.BlockSpec((2, depth, width), lambda i: (0, i, 0)),
            inside if narrow else pl.BlockSpec((depth, width), lambda i: (i, 0)),
            inside,
            inside if narrow else wide,
        ]
        + [ANYWHERE] * len(outs),
        out_specs=(wide, wide, wide, TOTAL),
        input_output_aliases={4 + i: i for i in range(len(outs))},
        cost_estimate=cost(rows, width, 30, 18),
        compiler_params=pltpu.CompilerParams(vmem_limit_bytes=16 * 2**20),
    )(pair, step, pair_other, part(old_other, (at, width)) if narrow else old_other, *outs)


def early(total, pair_other, grad, grad_other, first, second, other, old, old_other, width, outs):
    rows, cols = old.shape
    wide = columns(width)
    shape = jax.ShapeDtypeStruct((rows, cols), BF16)
    return pl.pallas_call(
        early_kernel,
        grid=(rows // STEP_ROWS,),
        out_shape=(shape, shape, shape),
        in_specs=[TOTAL, pl.BlockSpec((2, 16, 128), lambda i: (0, rows // 16, 0))] + [wide] * 5 + [columns(width // 2, width)] * 2 + [wide, wide] + [ANYWHERE] * 3,
        out_specs=(wide, wide, wide),
        input_output_aliases={11 + i: i for i in range(3)},
        cost_estimate=cost(rows, width, 60, 22),
    )(total, pair_other, grad, grad_other, first, second, other, other, grad_other, old, old_other, *outs)


def times(x, u):
    return lax.dot_general(x, u, (((0,), (0,)), ((), ())), preferred_element_type=F32)


def local_kernel(x_ref, u_ref, out_ref):
    out_ref[...] = times(x_ref[0], u_ref[...])


def local_product(x, u):
    blocks, depth, step = x.shape
    width = u.shape[1]
    return pl.pallas_call(
        local_kernel,
        grid=(blocks // 2,),
        out_shape=jax.ShapeDtypeStruct((blocks // 2 * step, width), F32),
        in_specs=[pl.BlockSpec((1, depth, step), lambda i: (i, 0, 0)), pl.BlockSpec((depth, width), lambda i: (0, 0))],
        out_specs=pl.BlockSpec((step, width), lambda i: (i, 0)),
        cost_estimate=SLIGHT,
        compiler_params=pltpu.CompilerParams(vmem_limit_bytes=32 * 2**20),
    )(x, u)


def finish_kernel(x_ref, u_ref, local_ref, *rest):
    grad_ref, squares_ref = rest[-2:]
    grad = local_ref[...] + times(x_ref[0], u_ref[...])
    grad_ref[...] = grad
    square = grad * grad
    lanes = sum(square[:, k : k + 128] for k in range(0, grad.shape[1], 128))

    @pl.when(pl.program_id(0) == 0)
    def _():
        squares_ref[...] = jnp.zeros_like(squares_ref)

    squares_ref[...] += jnp.sum(lanes.reshape(-1, 8, 128), axis=0)


def finish(x, u, local, earlier):
    blocks, depth, step = x.shape
    width = u.shape[1]
    rows = pl.BlockSpec((step, width), lambda i: (i, 0))
    return pl.pallas_call(
        finish_kernel,
        grid=(blocks // 2,),
        out_shape=(jax.ShapeDtypeStruct((blocks // 2 * step, width), F32), jax.ShapeDtypeStruct((8, 128), F32)),
        in_specs=[pl.BlockSpec((1, depth, step), lambda i: (blocks // 2 + i, 0, 0)), pl.BlockSpec((depth, width), lambda i: (0, 0)), rows] + [corner(value) for value in earlier],
        out_specs=(rows, pl.BlockSpec((8, 128), lambda i: (0, 0))),
        cost_estimate=SLIGHT,
        compiler_params=pltpu.CompilerParams(vmem_limit_bytes=32 * 2**20),
    )(x, u, local, *earlier)


EARLY = 256
UP = ((0, 768), (768, 768), (1536, 256))
FIRST = 2
LATE = ((256, 128), (384, 128), (512, 256), (1536, 128), (768, 384), (1152, 384), (1664, 128))


def part(value, piece):
    return value[:, piece[0] : piece[0] + piece[1]]


def holder(pieces, at):
    index = next(i for i, (start, width) in enumerate(pieces) if start <= at < start + width)
    return index, at - pieces[index][0]


def body(tokens, grad_out, weights, first_moment, second_moment):
    upstream, old = grad_out[0], weights[0]
    first, second = first_moment[0], second_moment[0]

    settled = settle(tokens[0])
    later = lax.optimization_barrier((upstream, settled))[0]
    up = [part(later if i else upstream, piece) for i, piece in enumerate(UP)]
    up_other = [swap_dp(piece) for piece in up]
    old_other = across(old)
    state_other = across(jnp.concatenate([first[:, :EARLY], second[:, : EARLY // 2]], axis=1))

    near, *leading = gate(
        (along_y(settled), part(first, LATE[FIRST]), part(second, LATE[FIRST])), (up_other[0],)
    )
    features = assemble(near, turned(near[:2], 1), turned(near[2:], 1))
    grads, squares = [], jnp.zeros((8, 128), F32)
    for i, (piece, other) in enumerate(zip(up, up_other)):
        grad, square = finish(features, other, local_product(features, piece), (old_other,) if i == 2 else ())
        grads.append(grad)
        squares = squares + square
    grad_other = across(jnp.concatenate([grads[0][:, :EARLY].astype(BF16), second[:, EARLY // 2 : EARLY]], axis=1))
    total = group_sum(squares, (state_other,))

    pairs, steps, received, flags = [], [], [], []
    outs = ()
    for i in range(len(LATE) + 2):
        if i < len(LATE):
            at, width = LATE[i]
            chunk, within = holder(UP, at)
            if i == FIRST:
                pair, step = make_first(total, grads[chunk], within, *leading), part(old, LATE[i])
            else:
                pair, step = make(total, grads[chunk], within, first, second, old, at, width)
            if i == 1:
                (pair,) = gate((pair,), (grad_other,))
            elif i > 3:
                earlier = [(received[0], received[1], flags[0]), (*received[2:4], *flags[1:2]), (*received[4:5], *flags[3:4])][i - 4]
                (pair,) = gate((pair,), earlier)
            pairs.append(pair)
            steps.append(step)
            received.append(across(pair))
        if i >= 2:
            j = i - 2
            at, width = LATE[j]
            *outs, flag = mix(pairs[j], steps[j], j != FIRST, received[j], old_other, at, width, old.shape, outs)
            flags.append(flag)
        if i == FIRST + 2:
            outs = early(total, received[FIRST], grads[0], grad_other, first, second, state_other, old, old_other, EARLY, outs)
    return tuple(out[None] for out in outs)


def solution(mesh):
    placed = P("replica", "dp", "tensor")
    return jax.shard_map(
        body,
        mesh=mesh,
        in_specs=(placed,) * 5,
        out_specs=(placed,) * 3,
        check_vma=False,
    )
```

```python
import functools

import jax
import jax.numpy as jnp
from jax import lax
from jax.experimental import pallas as pl
from jax.experimental.pallas import tpu as pltpu
from jax.sharding import PartitionSpec as P

D = 2048
FF = 14336
STEP = 1
FIX_ONE = 1.0 - 0.9**STEP
FIX_TWO = 1.0 - 0.95**STEP
BF16 = jnp.bfloat16
ANYWHERE = pl.BlockSpec(memory_space=pl.ANY)
SLIGHT = pl.CostEstimate(flops=0, bytes_accessed=4096, transcendentals=0)
F32 = jnp.float32


def across(value):
    return lax.ppermute(value, "replica", [(s, s ^ 4) for s in range(8)])


def swap_dp(value):
    return lax.ppermute(value, "dp", [(0, 1), (1, 0)])


def nothing_kernel(*refs):
    del refs


def corner(value):
    if value.ndim > 2:
        return pl.BlockSpec(memory_space=pltpu.VMEM)
    return pl.BlockSpec((1,) * (value.ndim - 2) + (16 if value.dtype == BF16 else 8, 128), lambda i: (0,) * value.ndim)


def gate(values, earlier, size=4096):
    return pl.pallas_call(
        nothing_kernel,
        grid=(1,),
        out_shape=[jax.ShapeDtypeStruct(value.shape, value.dtype) for value in values],
        in_specs=[ANYWHERE] * len(values) + [corner(value) for value in earlier],
        out_specs=[ANYWHERE] * len(values),
        input_output_aliases={i: i for i in range(len(values))},
        cost_estimate=pl.CostEstimate(flops=0, bytes_accessed=size, transcendentals=0),
        compiler_params=pltpu.CompilerParams(vmem_limit_bytes=4 * 2**20),
    )(*values, *earlier)


def turned(value, bits):
    return lax.ppermute(value, "tensor", [(t, t ^ bits) for t in range(8)])


def settle(mine):
    pairs = []
    for d in range(2):
        for t in range(8):
            stays = t // 4 == d
            pairs.append((d * 8 + t, d * 8 + t if stays else (1 - d) * 8 + (t ^ 6)))
    return lax.ppermute(mine, ("dp", "tensor"), pairs)


def along_y(value):
    copies = jnp.broadcast_to(value, (4, *value.shape))
    return lax.all_to_all(copies, "tensor", 0, 0, tiled=True, axis_index_groups=[[0, 2, 4, 6], [1, 3, 5, 7]])


def assemble_kernel(slot_ref, near_ref, low_ref, high_ref, out_ref):
    for k in range(4):
        out_ref[slot_ref[k]] = near_ref[k]
    for k in range(2):
        out_ref[slot_ref[4 + k]] = low_ref[k]
        out_ref[slot_ref[6 + k]] = high_ref[k]


def assemble(near, low, high):
    core = lax.axis_index("tensor") % 2
    flip = 4 * lax.axis_index("dp")
    places = jnp.stack([(2 * y + core) ^ flip for y in range(4)] + [(2 * y + 1 - core) ^ flip for y in range(4)])
    slots = places ^ (places // 4 * 2)
    whole = pl.BlockSpec(memory_space=pltpu.VMEM)
    return pl.pallas_call(
        assemble_kernel,
        out_shape=jax.ShapeDtypeStruct((8, *near.shape[1:]), BF16),
        in_specs=[pl.BlockSpec(memory_space=pltpu.SMEM)] + [whole] * 3,
        out_specs=whole,
        cost_estimate=SLIGHT,
        compiler_params=pltpu.CompilerParams(vmem_limit_bytes=24 * 2**20),
    )(slots.astype(jnp.int32), near, low, high)


def add_kernel(one_ref, two_ref, *rest):
    rest[-1][...] = one_ref[...] + two_ref[...]


def group_sum(value, earlier):
    value = value + turned(value, 1)
    value = value + turned(value, 2) + turned(value, 4) + turned(value, 6)
    return pl.pallas_call(
        add_kernel,
        grid=(1,),
        out_shape=jax.ShapeDtypeStruct(value.shape, F32),
        in_specs=[corner(value)] * 2 + [corner(item) for item in earlier],
        out_specs=corner(value),
        cost_estimate=SLIGHT,
        compiler_params=pltpu.CompilerParams(vmem_limit_bytes=4 * 2**20),
    )(value, swap_dp(value), *earlier)


def clip_of(total_ref):
    total = jnp.sum(total_ref[...], keepdims=True)
    return jnp.minimum(1.0, 1.0 / jnp.sqrt(total / (D * FF) + 1e-06))


def moments(scaled, first, second):
    one = 0.9 * first.astype(F32) + 0.1 * scaled
    two = 0.95 * second.astype(F32) + 0.05 * scaled * scaled
    return one.astype(BF16), two.astype(BF16)


def stepped(old, one, two):
    old = old.astype(F32)
    update = (one.astype(F32) * (1.0 / FIX_ONE)) / (jnp.sqrt(two.astype(F32) * (1.0 / FIX_TWO)) + 1e-08)
    return (old - 0.05 * (update + 0.1 * old)).astype(BF16)


def mean(a, b):
    return (0.5 * (a.astype(F32) + b.astype(F32))).astype(BF16)


def make_kernel(total_ref, grad_ref, first_ref, second_ref, old_ref, pair_ref, step_ref):
    one, two = moments(clip_of(total_ref) * grad_ref[...], first_ref[...], second_ref[...])
    pair_ref[0] = one
    pair_ref[1] = two
    step_ref[...] = stepped(old_ref[...], one, two)


def make_first_kernel(total_ref, grad_ref, first_ref, second_ref, pair_ref):
    rows = grad_ref.shape[0]
    clip = clip_of(total_ref)
    one, two = moments(clip * grad_ref[...], first_ref[...], second_ref[...])
    pair_ref[0, :rows] = one
    pair_ref[1, :rows] = two
    clip = jnp.broadcast_to(clip, (16, grad_ref.shape[1]))
    high = clip.astype(BF16)
    pair_ref[0, rows:] = high
    pair_ref[1, rows:] = (clip - high.astype(F32)).astype(BF16)


def make_first(total, grad, within, first, second):
    rows, width = first.shape
    chosen = lambda start: pl.BlockSpec((rows, width), lambda i: (0, start // width))
    return pl.pallas_call(
        make_first_kernel,
        grid=(1,),
        out_shape=jax.ShapeDtypeStruct((2, rows + 16, width), BF16),
        in_specs=[TOTAL, chosen(within), chosen(0), chosen(0)],
        out_specs=pl.BlockSpec((2, rows + 16, width), lambda i: (0, 0, 0)),
        cost_estimate=cost(rows, width, 30, 16),
        compiler_params=pltpu.CompilerParams(vmem_limit_bytes=24 * 2**20),
    )(total, grad, first, second)


def mix_kernel(ready, pair_ref, step_ref, pair_other_ref, old_other_ref, *rest):
    w_ref, one_ref, two_ref, flag_ref = rest[-4:]
    flag_ref[...] = jnp.zeros_like(flag_ref)
    depth = step_ref.shape[0]
    here = pl.ds(pl.multiple_of(pl.program_id(0) * depth, depth), depth)
    one_other, two_other = pair_other_ref[0, here], pair_other_ref[1, here]
    step = step_ref[...] if ready else stepped(step_ref[...], pair_ref[0], pair_ref[1])
    w_ref[...] = mean(step, stepped(old_other_ref[...], one_other, two_other))
    one_ref[...] = mean(pair_ref[0], one_other)
    two_ref[...] = mean(pair_ref[1], two_other)


def early_kernel(
    total_ref,
    clip_other_ref,
    grad_ref,
    grad_other_ref,
    first_ref,
    second_ref,
    first_other_ref,
    second_other_ref,
    second_rest_ref,
    old_ref,
    old_other_ref,
    *rest,
):
    w_ref, one_ref, two_ref = rest[-3:]
    one, two = moments(clip_of(total_ref) * grad_ref[...], first_ref[...], second_ref[...])
    second_other = jnp.concatenate([second_other_ref[...], second_rest_ref[...]], axis=1)
    clip_other = clip_other_ref[0, :1, :1].astype(F32) + clip_other_ref[1, :1, :1].astype(F32)
    scaled_other = clip_other * grad_other_ref[...].astype(F32)
    one_other, two_other = moments(scaled_other, first_other_ref[...], second_other)
    w_ref[...] = mean(stepped(old_ref[...], one, two), stepped(old_other_ref[...], one_other, two_other))
    one_ref[...] = mean(one, one_other)
    two_ref[...] = mean(two, two_other)


STEP_ROWS = 512
TOTAL = pl.BlockSpec((8, 128), lambda i: (0, 0))


def columns(width, at=0):
    return pl.BlockSpec((STEP_ROWS, width), lambda i: (i, at // width))


def pair_of(width):
    return pl.BlockSpec((2, STEP_ROWS, width), lambda i: (0, i, 0))


def cost(rows, width, flops, size):
    return pl.CostEstimate(flops=flops * rows * width, bytes_accessed=size * rows * width, transcendentals=0)


def make(total, grad, within, first, second, old, at, width):
    rows = grad.shape[0]
    wide = columns(width, at)
    return pl.pallas_call(
        make_kernel,
        grid=(rows // STEP_ROWS,),
        out_shape=(jax.ShapeDtypeStruct((2, rows, width), BF16), jax.ShapeDtypeStruct((rows, width), BF16)),
        in_specs=[TOTAL, columns(width, within), wide, wide, wide],
        out_specs=(pair_of(width), columns(width)),
        cost_estimate=cost(rows, width, 30, 16),
    )(total, grad, first, second, old)


def mix(pair, step, ready, pair_other, old_other, at, width, shape, outs):
    rows = shape[0]
    narrow = width == 128
    depth = rows if narrow else STEP_ROWS
    inside = pl.BlockSpec(memory_space=pltpu.VMEM)
    wide = pl.BlockSpec((depth, width), lambda i: (i, at // width))
    whole = jax.ShapeDtypeStruct(shape, BF16)
    return pl.pallas_call(
        functools.partial(mix_kernel, ready),
        grid=(rows // depth,),
        out_shape=(whole, whole, whole, jax.ShapeDtypeStruct((8, 128), F32)),
        in_specs=[
            inside if narrow else pl.BlockSpec((2, depth, width), lambda i: (0, i, 0)),
            inside if narrow else pl.BlockSpec((depth, width), lambda i: (i, 0)),
            inside,
            inside if narrow else wide,
        ]
        + [ANYWHERE] * len(outs),
        out_specs=(wide, wide, wide, TOTAL),
        input_output_aliases={4 + i: i for i in range(len(outs))},
        cost_estimate=cost(rows, width, 30, 18),
        compiler_params=pltpu.CompilerParams(vmem_limit_bytes=16 * 2**20),
    )(pair, step, pair_other, part(old_other, (at, width)) if narrow else old_other, *outs)


def early(total, pair_other, grad, grad_other, first, second, other, old, old_other, width, outs):
    rows, cols = old.shape
    wide = columns(width)
    shape = jax.ShapeDtypeStruct((rows, cols), BF16)
    return pl.pallas_call(
        early_kernel,
        grid=(rows // STEP_ROWS,),
        out_shape=(shape, shape, shape),
        in_specs=[TOTAL, pl.BlockSpec((2, 16, 128), lambda i: (0, rows // 16, 0))] + [wide] * 5 + [columns(width // 2, width)] * 2 + [wide, wide] + [ANYWHERE] * 3,
        out_specs=(wide, wide, wide),
        input_output_aliases={11 + i: i for i in range(3)},
        cost_estimate=cost(rows, width, 60, 22),
    )(total, pair_other, grad, grad_other, first, second, other, other, grad_other, old, old_other, *outs)


def times(x, u):
    return lax.dot_general(x, u, (((0,), (0,)), ((), ())), preferred_element_type=F32)


def local_kernel(x_ref, u_ref, out_ref):
    out_ref[...] = times(x_ref[0], u_ref[...])


def local_product(x, u):
    blocks, depth, step = x.shape
    width = u.shape[1]
    return pl.pallas_call(
        local_kernel,
        grid=(blocks // 2,),
        out_shape=jax.ShapeDtypeStruct((blocks // 2 * step, width), F32),
        in_specs=[pl.BlockSpec((1, depth, step), lambda i: (i, 0, 0)), pl.BlockSpec((depth, width), lambda i: (0, 0))],
        out_specs=pl.BlockSpec((step, width), lambda i: (i, 0)),
        cost_estimate=SLIGHT,
        compiler_params=pltpu.CompilerParams(vmem_limit_bytes=32 * 2**20),
    )(x, u)


def finish_kernel(x_ref, u_ref, local_ref, *rest):
    grad_ref, squares_ref = rest[-2:]
    grad = local_ref[...] + times(x_ref[0], u_ref[...])
    grad_ref[...] = grad
    square = grad * grad
    lanes = sum(square[:, k : k + 128] for k in range(0, grad.shape[1], 128))

    @pl.when(pl.program_id(0) == 0)
    def _():
        squares_ref[...] = jnp.zeros_like(squares_ref)

    squares_ref[...] += jnp.sum(lanes.reshape(-1, 8, 128), axis=0)


def finish_inside_kernel(x_ref, u_ref, local_ref, *rest):
    grad_ref, squares_ref = rest[-2:]
    blocks, _, step = x_ref.shape
    total = jnp.zeros(squares_ref.shape, F32)
    for k in range(blocks // 2):
        here = slice(k * step, (k + 1) * step)
        grad = local_ref[here] + times(x_ref[blocks // 2 + k], u_ref[...])
        grad_ref[here] = grad
        square = grad * grad
        lanes = sum(square[:, j : j + 128] for j in range(0, grad.shape[1], 128))
        total = total + jnp.sum(lanes.reshape(-1, 8, 128), axis=0)
    squares_ref[...] = total


def finish_inside(x, u, local, earlier):
    inside = pl.BlockSpec(memory_space=pltpu.VMEM)
    return pl.pallas_call(
        finish_inside_kernel,
        grid=(1,),
        out_shape=(jax.ShapeDtypeStruct(local.shape, F32), jax.ShapeDtypeStruct((8, 128), F32)),
        in_specs=[inside] * 3 + [corner(value) for value in earlier],
        out_specs=(inside, inside),
        cost_estimate=SLIGHT,
        compiler_params=pltpu.CompilerParams(vmem_limit_bytes=32 * 2**20),
    )(x, u, local, *earlier)


def finish(x, u, local, earlier):
    blocks, depth, step = x.shape
    width = u.shape[1]
    rows = pl.BlockSpec((step, width), lambda i: (i, 0))
    return pl.pallas_call(
        finish_kernel,
        grid=(blocks // 2,),
        out_shape=(jax.ShapeDtypeStruct((blocks // 2 * step, width), F32), jax.ShapeDtypeStruct((8, 128), F32)),
        in_specs=[pl.BlockSpec((1, depth, step), lambda i: (blocks // 2 + i, 0, 0)), pl.BlockSpec((depth, width), lambda i: (0, 0)), rows] + [corner(value) for value in earlier],
        out_specs=(rows, pl.BlockSpec((8, 128), lambda i: (0, 0))),
        cost_estimate=SLIGHT,
        compiler_params=pltpu.CompilerParams(vmem_limit_bytes=32 * 2**20),
    )(x, u, local, *earlier)


EARLY = 256
UP = ((0, 768), (768, 768), (1536, 256))
FIRST = 2
LATE = ((256, 128), (384, 128), (512, 256), (1536, 128), (768, 384), (1152, 384), (1664, 128))


def part(value, piece):
    return value[:, piece[0] : piece[0] + piece[1]]


def holder(pieces, at):
    index = next(i for i, (start, width) in enumerate(pieces) if start <= at < start + width)
    return index, at - pieces[index][0]


def body(tokens, grad_out, weights, first_moment, second_moment):
    upstream, old = grad_out[0], weights[0]
    first, second = first_moment[0], second_moment[0]

    settled = settle(tokens[0])
    later = lax.optimization_barrier((upstream, settled))[0]
    up = [part(later if i else upstream, piece) for i, piece in enumerate(UP)]
    up_other = [swap_dp(piece) for piece in up]
    old_other = across(old)
    state_other = across(jnp.concatenate([first[:, :EARLY], second[:, : EARLY // 2]], axis=1))

    near, *leading = gate(
        (along_y(settled), part(first, LATE[FIRST]), part(second, LATE[FIRST])), (up_other[0],)
    )
    features = assemble(near, turned(near[:2], 1), turned(near[2:], 1))
    grads, squares = [], jnp.zeros((8, 128), F32)
    for i, (piece, other) in enumerate(zip(up, up_other)):
        grad, square = (finish_inside if i == 2 else finish)(features, other, local_product(features, piece), (old_other,) if i == 2 else ())
        grads.append(grad)
        squares = squares + square
    grad_other = across(jnp.concatenate([grads[0][:, :EARLY].astype(BF16), second[:, EARLY // 2 : EARLY]], axis=1))
    total = group_sum(squares, (state_other,))

    pairs, steps, received, flags = [], [], [], []
    outs = ()
    for i in range(len(LATE) + 2):
        if i < len(LATE):
            at, width = LATE[i]
            chunk, within = holder(UP, at)
            if i == FIRST:
                pair, step = make_first(total, grads[chunk], within, *leading), part(old, LATE[i])
            else:
                pair, step = make(total, grads[chunk], within, first, second, old, at, width)
            if i == 1:
                (pair,) = gate((pair,), (grad_other,))
            elif i > 3:
                earlier = [(received[0], received[1], flags[0]), (*received[2:4], *flags[1:2]), (*received[4:5], *flags[3:4])][i - 4]
                (pair,) = gate((pair,), earlier)
            pairs.append(pair)
            steps.append(step)
            received.append(across(pair))
        if i >= 2:
            j = i - 2
            at, width = LATE[j]
            *outs, flag = mix(pairs[j], steps[j], j != FIRST, received[j], old_other, at, width, old.shape, outs)
            flags.append(flag)
        if i == FIRST + 2:
            outs = early(total, received[FIRST], grads[0], grad_other, first, second, state_other, old, old_other, EARLY, outs)
    return tuple(out[None] for out in outs)


def solution(mesh):
    placed = P("replica", "dp", "tensor")
    return jax.shard_map(
        body,
        mesh=mesh,
        in_specs=(placed,) * 5,
        out_specs=(placed,) * 3,
        check_vma=False,
    )
```
